128 devices in a mesh: dp: 128 (over y, z, x, core).
Axes of the slice: x: 4, y: 4, z: 4, core: 2. Of those that a mesh axis runs over, the one named last changes fastest.
Arguments:
- buffer_small: bfloat16 [2048, 8, 8, 640], P('dp'), may hold values from -6 to 6
- buffer_large: bfloat16 [1024, 12, 12, 640], P('dp'), may hold values from -6 to 6
- fetch_small: int32 [256], P('dp'), may hold values from 0 to 15, as said below
- fetch_large: int32 [128], P('dp'), may hold values from 0 to 7, as said below
- reinit_small: int32 [256], P('dp'), may hold values 0 or 1
- reinit_large: int32 [128], P('dp'), may hold values 0 or 1
- fresh_small: bfloat16 [256, 8, 8, 640], P('dp'), may hold values from -1 to 1
- fresh_large: bfloat16 [128, 12, 12, 640], P('dp'), may hold values from -1 to 1
- noise_small: bfloat16 [2, 256, 8, 8, 640], P(None, 'dp'), may hold values from -2 to 2
- noise_large: bfloat16 [2, 128, 12, 12, 640], P(None, 'dp'), may hold values from -2 to 2
- probe_small: bfloat16 [256, 8, 8, 640], P('dp'), may hold values from -6 to 6
- probe_large: bfloat16 [128, 12, 12, 640], P('dp'), may hold values from -6 to 6
- train_maps: bfloat16 [512, 12, 12, 640], P('dp'), may hold values from -6 to 6
- train_group: int32 [512], P('dp'), may hold values 0 or 1
- train_cot: bfloat16 [512, 12, 12, 640], P('dp'), may hold values from -6 to 6
- kernel_one: bfloat16 [3, 3, 640, 640], replicated, may hold values from -0.078125 to 0.078125
- bias_one: float32 [640], replicated, may hold values from -3 to 3
- kernel_two: bfloat16 [3, 3, 640, 640], replicated, may hold values from -0.078125 to 0.078125
- bias_two: float32 [640], replicated, may hold values from -3 to 3
Outputs:
- samples_small: bfloat16 [256, 8, 8, 640], P('dp')
- samples_large: bfloat16 [128, 12, 12, 640], P('dp')
- buffer_small_new: bfloat16 [2048, 8, 8, 640], P('dp')
- buffer_large_new: bfloat16 [1024, 12, 12, 640], P('dp')
- train_out: bfloat16 [512, 12, 12, 640], P('dp')
- train_grad: float32 [512, 12, 12, 640], P('dp')
- grad_kernel_one: float32 [3, 3, 640, 640], replicated
- grad_bias_one: float32 [640], replicated
- grad_kernel_two: float32 [3, 3, 640, 640], replicated
- grad_bias_two: float32 [640], replicated
The draws below stay inside these ranges and needn't reach their ends.
Inputs may be any that keep to these rules, and one draw needn't show every extreme that they name: `fetch_small`: within each aligned block of 2 entries that starts at a multiple of 2, the numbers are distinct. `fetch_large`: within each aligned block of 1 entries that starts at a multiple of 1, the numbers are distinct.
All inputs are finite; a program needn't handle non-finite values. No bound on the sum of `reinit_small` or of `reinit_large` or of `train_group` on one device may be relied on, other than what follows from the above.
Results may differ from the reference program's by a relative error of at most 0.0057.
Values may be sent and summed in bfloat16 or wider, within the bound.
A program may use at most 256 MiB of HBM per device.

```python
import jax
import jax.numpy as jnp
from jax import lax

C = 640
SMALL_SIDE = 8
LARGE_SIDE = 12
STEPS = 2
CH8_DEV = 2
CH12_DEV = 1
B8_DEV = 16
B12_DEV = 8
TRAIN = 512
CH8 = 256
CH12 = 128
B8 = 2048
B12 = 1024
N_DP = 128


def pick_rows(key, owners, per_owner, owner_rows):
    keys = jax.random.split(key, owners)
    chosen = jax.vmap(lambda single: jax.random.permutation(single, owner_rows)[:per_owner])(keys)
    return chosen.reshape(-1).astype(jnp.int32)


def draw_fetch_small(key, part):
    key = jax.random.fold_in(key, 11)
    return pick_rows(key, CH8 // CH8_DEV, CH8_DEV, B8_DEV)


def draw_fetch_large(key, part):
    key = jax.random.fold_in(key, 23)
    return pick_rows(key, CH12 // CH12_DEV, CH12_DEV, B12_DEV)


def touch_ends(entries, key, low, high):
    longest = entries.shape.index(max(entries.shape))
    spots = []
    for shift in (0, 1):
        where = [jax.random.randint(jax.random.fold_in(key, axis), (), 0, length) for axis, length in enumerate(entries.shape)]
        where[longest] = (where[longest] + shift) % entries.shape[longest]
        spots.append(tuple(where))
    return entries.at[spots[0]].set(low).at[spots[1]].set(high)


def steps_of(stream_key, dims, shards, low, top_value):
    def one(dim, blocks):
        steps = jax.random.uniform(jax.random.fold_in(jax.random.fold_in(stream_key, 6), dim), (blocks,), jnp.float32, low / len(shards), top_value / len(shards))
        return jnp.repeat(jnp.exp(steps), dims[dim] // blocks).reshape((-1,) + (1,) * (len(dims) - dim - 1))

    loudness = one(*shards[0])
    for cut in shards[1:]:
        loudness = loudness * one(*cut)
    return loudness


def bell_draw(key, dims, deviation, reach, cuts=(), held_as=jnp.bfloat16):
    drawn = deviation * jax.random.normal(key, dims, jnp.float32)
    if cuts:
        drawn = drawn * steps_of(key, dims, cuts, -0.22, 0.18)
    return jnp.clip(drawn, -reach, reach).astype(held_as)


def setup_inputs(seed: int = 0) -> dict:
    streams_of = jax.random.split(jax.random.key(seed), 20)
    return {
        "buffer_small": bell_draw(streams_of[0], (B8, SMALL_SIDE, SMALL_SIDE, C), 1.0, 6.0, ((0, 128),)),
        "buffer_large": bell_draw(streams_of[1], (B12, LARGE_SIDE, LARGE_SIDE, C), 1.0, 6.0, ((0, 128),)),
        "fetch_small": draw_fetch_small(jax.random.fold_in(streams_of[19], 71), 0),
        "fetch_large": draw_fetch_large(jax.random.fold_in(streams_of[19], 71), 0),
        "reinit_small": touch_ends((jax.random.randint(streams_of[4], (CH8,), 0, 4) < 1).astype(jnp.int32), jax.random.fold_in(streams_of[4], 1), 0, 1),
        "reinit_large": touch_ends((jax.random.randint(streams_of[5], (CH12,), 0, 4) < 1).astype(jnp.int32), jax.random.fold_in(streams_of[5], 1), 0, 1),
        "fresh_small": jnp.clip(jax.random.uniform(streams_of[6], (CH8, SMALL_SIDE, SMALL_SIDE, C), jnp.float32, -1.0, 1.0) * steps_of(streams_of[6], (CH8, SMALL_SIDE, SMALL_SIDE, C), ((0, 128),), -0.4, 0.0), -1.0, 1.0).astype(jnp.bfloat16),
        "fresh_large": jnp.clip(jax.random.uniform(streams_of[7], (CH12, LARGE_SIDE, LARGE_SIDE, C), jnp.float32, -1.0, 1.0) * steps_of(streams_of[7], (CH12, LARGE_SIDE, LARGE_SIDE, C), ((0, 128),), -0.4, 0.0), -1.0, 1.0).astype(jnp.bfloat16),
        "noise_small": bell_draw(streams_of[8], (STEPS, CH8, SMALL_SIDE, SMALL_SIDE, C), 0.3, 2.0, ((1, 128),)),
        "noise_large": bell_draw(streams_of[9], (STEPS, CH12, LARGE_SIDE, LARGE_SIDE, C), 0.3, 2.0, ((1, 128),)),
        "probe_small": bell_draw(streams_of[10], (CH8, SMALL_SIDE, SMALL_SIDE, C), 1.0, 6.0, ((0, 128),)),
        "probe_large": bell_draw(streams_of[11], (CH12, LARGE_SIDE, LARGE_SIDE, C), 1.0, 6.0, ((0, 128),)),
        "train_maps": bell_draw(streams_of[12], (TRAIN, LARGE_SIDE, LARGE_SIDE, C), 1.0, 6.0, ((0, 128),)),
        "train_group": touch_ends((jax.random.randint(streams_of[13], (TRAIN,), 0, 2) < 1).astype(jnp.int32), jax.random.fold_in(streams_of[13], 1), 0, 1),
        "train_cot": bell_draw(streams_of[14], (TRAIN, LARGE_SIDE, LARGE_SIDE, C), 1.0, 6.0, ((0, 128),)),
        "kernel_one": bell_draw(streams_of[15], (3, 3, C, C), (9 * C) ** -0.5, 0.078125),
        "bias_one": bell_draw(streams_of[16], (C,), 0.5, 3.0, (), jnp.float32),
        "kernel_two": bell_draw(streams_of[17], (3, 3, C, C), (9 * C) ** -0.5, 0.078125),
        "bias_two": bell_draw(streams_of[18], (C,), 0.5, 3.0, (), jnp.float32),
    }


sgld_step = 1.0

@jax.custom_vjp
def low(v):
    return lax.optimization_barrier(v.astype(jnp.bfloat16)).astype(jnp.float32)

@jax.custom_vjp
def low_back(v):
    return v

def low_keep(v):
    return (low(v), None)

def low_pass(kept, grad):
    return (grad,)

def back_keep(v):
    return (v, None)

def back_low(kept, grad):
    return (low(grad),)
low.defvjp(low_keep, low_pass)
low_back.defvjp(back_keep, back_low)

def convolve(field_map, kernel):
    return lax.conv_general_dilated(field_map, kernel, (1, 1), 'SAME', dimension_numbers=('NHWC', 'HWIO', 'NHWC'), precision=lax.Precision.HIGHEST)

def residual_block(inputs, region, kernel_one, bias_one, kernel_two, bias_two):
    act_in = low(jax.nn.silu(inputs) * region)
    pre_one = low_back(convolve(act_in, kernel_one) + bias_one)
    act_mid = low(jax.nn.silu(pre_one) * region)
    pre_two = low_back(convolve(act_mid, kernel_two) + bias_two)
    return (inputs + pre_two) * region

def region_of(groups, extent, inner_side):
    positions = jnp.arange(extent)
    inside = (positions[:, None] < inner_side) & (positions[None, :] < inner_side)
    kept_cells = (groups[:, None, None] == 1) | inside[None]
    return kept_cells.astype(jnp.float32)[..., None]

def source_rows(fetch_rows, per_device, slot_base, total_slots, owner_rows):
    chains = jnp.arange(fetch_rows.shape[0], dtype=jnp.int32)
    device_of = chains // per_device
    slot_of = chains % per_device
    distance = (2 * (slot_of + slot_base) + 1) * N_DP // (2 * total_slots)
    owner = (device_of - distance) % N_DP
    return owner * owner_rows + jnp.take(fetch_rows, owner * per_device + slot_of)

def chain_run(starts, probe_map, noises, weights):
    region = jnp.ones(starts.shape[:3] + (1,), jnp.float32)
    cotangent = probe_map.astype(jnp.float32)

    def energy(inputs):
        return residual_block(inputs, region, weights[0], weights[1], weights[2], weights[3])
    chain_state = starts
    for step_index in range(STEPS):
        pull = jax.vjp(energy, chain_state)[1]
        chain_state = chain_state + sgld_step * pull(cotangent)[0] + noises[step_index].astype(jnp.float32)
    return chain_state

def reference(buffer_small, buffer_large, fetch_small, fetch_large, reinit_small, reinit_large, fresh_small, fresh_large, noise_small, noise_large, probe_small, probe_large, train_maps, train_group, train_cot, kernel_one, bias_one, kernel_two, bias_two):
    weights = (kernel_one.astype(jnp.float32), bias_one, kernel_two.astype(jnp.float32), bias_two)
    total_slots = CH8_DEV + CH12_DEV
    rows_small = source_rows(fetch_small, CH8_DEV, 0, total_slots, B8_DEV)
    rows_large = source_rows(fetch_large, CH12_DEV, CH8_DEV, total_slots, B12_DEV)
    start_small = jnp.where(reinit_small[:, None, None, None] == 1, fresh_small.astype(jnp.float32), buffer_small[rows_small].astype(jnp.float32))
    start_large = jnp.where(reinit_large[:, None, None, None] == 1, fresh_large.astype(jnp.float32), buffer_large[rows_large].astype(jnp.float32))
    samples_small = chain_run(start_small, probe_small, noise_small, weights).astype(jnp.bfloat16)
    samples_large = chain_run(start_large, probe_large, noise_large, weights).astype(jnp.bfloat16)
    buffer_small_new = buffer_small.at[rows_small].set(samples_small)
    buffer_large_new = buffer_large.at[rows_large].set(samples_large)
    pieces = (train_maps.reshape((N_DP, -1) + train_maps.shape[1:]), train_group.reshape(N_DP, -1), train_cot.reshape((N_DP, -1) + train_cot.shape[1:]))

    def train_piece(totals, map_piece):
        region = region_of(map_piece[1], LARGE_SIDE, SMALL_SIDE)

        def forward(inputs, first_kernel, first_bias, second_kernel, second_bias):
            return residual_block(inputs, region, first_kernel, first_bias, second_kernel, second_bias)
        outputs, pull = jax.vjp(forward, map_piece[0].astype(jnp.float32), weights[0], weights[1], weights[2], weights[3])
        grads = pull(map_piece[2].astype(jnp.float32))
        totals = (totals[0] + grads[1], totals[1] + grads[2], totals[2] + grads[3], totals[3] + grads[4])
        return (totals, (outputs.astype(jnp.bfloat16), grads[0]))
    zero_sums = (jnp.zeros(weights[0].shape, jnp.float32), jnp.zeros(weights[1].shape, jnp.float32), jnp.zeros(weights[2].shape, jnp.float32), jnp.zeros(weights[3].shape, jnp.float32))
    totals, mapped = lax.scan(train_piece, zero_sums, pieces)
    train_out = mapped[0].reshape(train_maps.shape)
    train_grad = mapped[1].reshape(train_maps.shape)
    return (samples_small, samples_large, buffer_small_new, buffer_large_new, train_out, train_grad, totals[0], totals[1], totals[2], totals[3])
```

```python
import functools

import jax
import jax.numpy as jnp
from jax import lax
from jax.experimental import pallas as pl
from jax.experimental.pallas import tpu as pltpu
from jax.sharding import PartitionSpec as P

MESH = pl.DeviceIdType.MESH
F32 = jnp.float32
BF16 = jnp.bfloat16

BLK = 240
STRIDES = (2, 8, 32)


class Place:
    def __init__(self):
        me = lax.axis_index("dp")
        self.me = me
        self.core = lax.rem(me, 2)
        self.sib = me + 1 - 2 * self.core
        self.coord = [lax.rem(me // s, 4) for s in STRIDES]

    def near(self, axis, step):
        m = self.coord[axis]
        return self.me + (lax.rem(m + step, 4) - m) * STRIDES[axis]


class Copy:
    def __init__(self, **fields):
        self.fields = fields

    def made(self):
        return pltpu.make_async_remote_copy(**self.fields)

    started = []

    def start(self):
        self.made().start()
        Copy.started.append(self)

    def wait(self):
        self.made().wait()

    def wait_send(self):
        self.made().wait_send()

    def wait_recv(self):
        self.made().wait_recv()


def rows_loop(total, step, body):
    def run(i, carry):
        body(pl.multiple_of(i * step, step))
        return carry
    lax.fori_loop(0, total // step, run, 0)


class Reduce:
    def __init__(self, place, g, sib, r1, r1o, r2, r3, q1, q2, a2, bias, out, bias_out, sends, recvs, local):
        self.__dict__.update(locals())
        self.kinds = {}

    def axes(self, p):
        return [p, (p + 1) % 3, (p + 2) % 3]

    def copy(self, c, p, kind, src, dst, dev):
        k = self.kinds.setdefault(kind, len(self.kinds))
        return Copy(src_ref=src, dst_ref=dst, send_sem=self.sends.at[c, p, k], recv_sem=self.recvs.at[c, p, k],
                    device_id=(dev,), device_id_type=MESH)

    def d0(self, c, p):
        P = self.place
        return self.copy(c, p, "core", self.g.at[c, p, 1 - P.core], self.sib.at[c, p], P.sib)

    def d1(self, c, p):
        P = self.place
        ax = self.axes(p)[0]
        m = P.coord[ax]
        R, L, O = [lax.rem(m + d, 4) for d in (1, 3, 2)]
        dr, dl = P.near(ax, 1), P.near(ax, 3)
        h0, h1 = pl.ds(0, 128), pl.ds(128, 112)
        h = self.sib
        return dict(
            or_=self.copy(c, p, "1or", h.at[c, p, O, h0], self.r1o.at[c, p, 0], dr),
            ol=self.copy(c, p, "1ol", h.at[c, p, O, h1], self.r1o.at[c, p, 1, pl.ds(0, 112)], dl),
            ra=self.copy(c, p, "1ra", h.at[c, p, R, h1], self.r1.at[c, p, 0, h1], dr),
            la=self.copy(c, p, "1la", h.at[c, p, L, h0], self.r1.at[c, p, 1, h0], dl),
            rb=self.copy(c, p, "1rb", h.at[c, p, R, h0], self.r1.at[c, p, 0, h0], dr),
            lb=self.copy(c, p, "1lb", h.at[c, p, L, h1], self.r1.at[c, p, 1, h1], dl),
        )

    def d2(self, c, p):
        P = self.place
        ax = self.axes(p)[1]
        m = P.coord[ax]
        return [self.copy(c, p, "2" + str(s), self.q1.at[c, p, lax.rem(m + s, 4)], self.r2.at[c, p, s - 1], P.near(ax, s))
                for s in (2, 1, 3)]

    def d3(self, c, p):
        P = self.place
        ax = self.axes(p)[2]
        m = P.coord[ax]
        return [self.copy(c, p, "3" + str(s), self.q2.at[c, p, lax.rem(m + s, 4)], self.r3.at[c, p, s - 1], P.near(ax, s))
                for s in (2, 1, 3)]

    def e3(self, c, p):
        P = self.place
        a1, a2 = self.axes(p)[1:]
        mine = self.a2.at[c, p, P.coord[a1], P.coord[a2]]
        return [self.copy(c, p, "e3" + str(s), mine, mine, P.near(a2, s)) for s in (2, 1, 3)]

    def e2(self, c, p):
        P = self.place
        ax = self.axes(p)[1]
        mine = self.a2.at[c, p, P.coord[ax]]
        return [self.copy(c, p, "e2" + str(s), mine, mine, P.near(ax, s)) for s in (2, 1, 3)]

    def e1(self, c, p):
        P = self.place
        ax = self.axes(p)[0]
        m = P.coord[ax]
        dr, dl = P.near(ax, 1), P.near(ax, 3)
        R, L, O = [lax.rem(m + d, 4) for d in (1, 3, 2)]
        o = self.out
        core = P.core
        h0, h1 = pl.ds(0, 128), pl.ds(128, 112)
        block = lambda b: o.at[c, p, core, b]
        part = lambda b, h: o.at[c, p, core, b, h]
        src = self.fin.at[c, p]
        cp = functools.partial(self.copy, c, p)
        return dict(
            r=cp("e1r", src, block(m), dr),
            l=cp("e1l", src, block(m), dl),
            s=cp("e1s", src, block(m), P.sib),
            fr=cp("e1fr", part(L, h0), part(L, h0), dr),
            fl=cp("e1fl", part(R, h1), part(R, h1), dl),
            sr=cp("e1sr", block(R), block(R), P.sib),
            sl=cp("e1sl", block(L), block(L), P.sib),
            so0=cp("e1so0", part(O, h0), part(O, h0), P.sib),
            so1=cp("e1so1", part(O, h1), part(O, h1), P.sib),
        )

    def p0(self, c):
        for p in range(3):
            self.d0(c, p).start()

    def p0w(self, c):
        P = self.place
        for p in range(3):
            self.d0(c, p).wait_recv()

            def add(i, carry, p=p):
                b = lax.rem(i, 4)
                rows = pl.ds(pl.multiple_of((i // 4) * 48, 16), 48)
                self.sib[c, p, b, rows, :] = (
                    self.sib[c, p, b, rows, :].astype(F32) + self.g[c, p, P.core, b, rows, :].astype(F32)
                ).astype(BF16)
                return carry
            lax.fori_loop(0, 20, add, 0)

    def p1a(self, c):
        for p in range(3):
            d = self.d1(c, p)
            for k in ("or_", "ol", "ra", "la"):
                d[k].start()

    def p1b(self, c):
        P = self.place
        for p in range(3):
            d = self.d1(c, p)
            m = P.coord[self.axes(p)[0]]
            R, L = lax.rem(m + 1, 4), lax.rem(m + 3, 4)
            h = self.sib
            d["or_"].wait_recv()

            def addr(r0):
                rows = pl.ds(r0, 64)
                h[c, p, R, rows, :] = (h[c, p, R, rows, :].astype(F32) + self.r1o[c, p, 0, rows, :].astype(F32)).astype(BF16)
            rows_loop(128, 64, addr)
            d["rb"].start()
            d["ol"].wait_recv()

            def addl(r0):
                rows = pl.ds(r0, 16)
                to = pl.ds(pl.multiple_of(r0 + 128, 16), 16)
                h[c, p, L, to, :] = (h[c, p, L, to, :].astype(F32) + self.r1o[c, p, 1, rows, :].astype(F32)).astype(BF16)
            rows_loop(112, 16, addl)
            d["lb"].start()

    def v1(self, c, p, rows):
        P = self.place
        m = P.coord[self.axes(p)[0]]
        return (self.sib[c, p, m, rows, :].astype(F32)
                + self.r1[c, p, 0, rows, :].astype(F32) + self.r1[c, p, 1, rows, :].astype(F32))

    def p1c(self, c):
        for p in range(3):
            d = self.d1(c, p)
            for k in ("ra", "la", "rb", "lb"):
                d[k].wait_recv()

            def add(r0):
                b = r0 // 64
                inner = pl.multiple_of(r0 - b * 64, 16)
                self.q1[c, p, b, pl.ds(inner, 16), :] = self.v1(c, p, pl.ds(r0, 16)).astype(BF16)
            rows_loop(240, 16, add)
            self.q1[c, p, 3, 48:64, :] = jnp.zeros((16, 640), BF16)

    def send(self, which, c):
        for p in range(3):
            for k in which(c, p):
                k.start()

    def receive(self, which, c):
        for p in range(3):
            for k in which(c, p):
                k.wait_recv()

    def p2a(self, c):
        self.send(self.d2, c)

    def v2(self, c, p, b):
        P = self.place
        m = P.coord[self.axes(p)[1]]
        rows = pl.ds(pl.multiple_of(b * 16, 16), 16)
        total = self.q1[c, p, m, rows, :].astype(F32)
        for s in range(3):
            total = total + self.r2[c, p, s, rows, :].astype(F32)
        return total

    def p2c(self, c):
        for p in range(3):
            for k in self.d2(c, p):
                k.wait_recv()

            def add(b, carry, p=p):
                self.q2[c, p, b] = self.v2(c, p, b).astype(BF16)
                return carry
            lax.fori_loop(0, 4, add, 0)

    def p3a(self, c):
        self.send(self.d3, c)

    def p3c(self, c):
        P = self.place
        for p in range(3):
            for k in self.d3(c, p):
                k.wait_recv()
            m2, m = P.coord[self.axes(p)[1]], P.coord[self.axes(p)[2]]
            total = self.v2(c, p, m)
            for s in range(3):
                total = total + self.r3[c, p, s].astype(F32)
            self.a2[c, p, m2, m] = total.astype(BF16)

    def e3a(self, c):
        self.send(self.e3, c)

    def e3c(self, c):
        self.receive(self.e3, c)

    def e2a(self, c):
        self.send(self.e2, c)

    def e2c(self, c):
        self.receive(self.e2, c)

    def e1a(self, c):
        P = self.place
        for p in range(3):
            for b in range(4):
                n = 4 if b < 3 else 3
                for i in range(n):
                    self.fin[c, p, pl.ds(b * 64 + i * 16, 16), :] = self.a2[c, p, b, i]
            e = self.e1(c, p)
            e["r"].start()
            e["l"].start()
            e["s"].start()
            m = P.coord[self.axes(p)[0]]
            pltpu.make_async_copy(self.fin.at[c, p], self.out.at[c, p, P.core, m], self.local.at[c, p]).start()

    def e1b(self, c):
        for p in range(3):
            e = self.e1(c, p)
            e["r"].wait_recv()
            e["fr"].start()
            e["sl"].start()
            e["l"].wait_recv()
            e["fl"].start()
            e["sr"].start()

    def e1c(self, c):
        for p in range(3):
            e = self.e1(c, p)
            e["fr"].wait_recv()
            e["so0"].start()
            e["fl"].wait_recv()
            e["so1"].start()

    def end(self, c):
        P = self.place
        for p in range(3):
            e = self.e1(c, p)
            for k in ("s", "sr", "sl", "so0", "so1"):
                e[k].wait_recv()
            m = P.coord[self.axes(p)[0]]
            pltpu.make_async_copy(self.fin.at[c, p], self.out.at[c, p, P.core, m], self.local.at[c, p]).wait()

    def bias_peers(self, level):
        P = self.place
        if level == 0:
            return [(0, P.sib, P.core)]
        ax = level - 1
        return [(s, P.near(ax, s), P.coord[ax]) for s in (1, 2, 3)]

    def bias_copies(self, level):
        return [self.copy(0, 0, "b%d%d" % (level, s), self.bias.at[level, slot], self.bias.at[level, slot], dev)
                for s, dev, slot in self.bias_peers(level)]

    def ba(self, level):
        for k in self.bias_copies(level):
            k.start()

    def bb(self, level):
        for k in self.bias_copies(level):
            k.wait_recv()
        total = self.bias[level, 0] + self.bias[level, 1]
        if level:
            total = total + self.bias[level, 2] + self.bias[level, 3]
        if level < 3:
            self.bias[level + 1, self.place.coord[level]] = total
        else:
            self.bias_out[...] = total

    def drain(self, c):
        for k in Copy.started:
            k.wait_send()
        Copy.started.clear()


def entry_barrier(P):
    barrier = pltpu.get_barrier_semaphore()
    who = [P.near(a, s) for a in range(3) for s in (1, 2, 3)] + [P.sib]
    for w in who:
        pl.semaphore_signal(barrier, inc=1, device_id=(w,), device_id_type=MESH)
    pl.semaphore_wait(barrier, len(who))


KINDS = 48


def reduce_scratch(chunks=2):
    v = lambda *s: pltpu.VMEM(s, BF16)
    return dict(
        sib=v(chunks, 3, 4, 240, 640), r1=v(chunks, 3, 2, 240, 640), r1o=v(chunks, 3, 2, 128, 640),
        r2=v(chunks, 3, 3, 64, 640), r3=v(chunks, 3, 3, 16, 640),
        q1=v(chunks, 3, 4, 64, 640), q2=v(chunks, 3, 4, 16, 640), a2=v(chunks, 3, 4, 4, 16, 640),
        fin=v(chunks, 3, 240, 640), bias=pltpu.VMEM((4, 4, 8, 640), F32),
        sends=pltpu.SemaphoreType.DMA((chunks, 3, KINDS)), recvs=pltpu.SemaphoreType.DMA((chunks, 3, KINDS)),
        local=pltpu.SemaphoreType.DMA((chunks, 3)),
    )

ORDER2 = [("ba", 0), ("p0", 0), ("p0", 1), ("bb", 0), ("ba", 1), ("p0w", 0), ("p1a", 0), ("p0w", 1), ("p1b", 0), ("p1a", 1), ("bb", 1), ("ba", 2), ("p1c", 0), ("p2a", 0), ("bb", 2), ("ba", 3),
          ("p2c", 0), ("p3a", 0), ("p3c", 0), ("e3a", 0), ("bb", 3), ("e3c", 0), ("e2a", 0),
          ("p1b", 1), ("e2c", 0), ("e1a", 0), ("p1c", 1), ("p2a", 1), ("p2c", 1), ("p3a", 1), ("e1b", 0), ("p3c", 1),
          ("e3a", 1), ("e3c", 1), ("e2a", 1), ("e1c", 0), ("e2c", 1), ("e1a", 1), ("e1b", 1), ("e1c", 1), ("end", 0), ("end", 1), ("drain", 0)]


def ar_kernel(order, names, g_hbm, bias_in, out, bias_out, gin, *scr):
    refs = dict(zip(names, scr))
    P = Place()
    Copy.started.clear()
    copies = [pltpu.make_async_copy(g_hbm.at[c], gin.at[c], refs["local"].at[c, 0]) for c in range(2)]
    for cp in copies:
        cp.start()
    refs["bias"][0, P.core] = bias_in[...]
    entry_barrier(P)
    for cp in copies:
        cp.wait()
    red = Reduce(P, gin, **{k: refs[k] for k in names if k not in ("fin",)}, out=out, bias_out=bias_out)
    red.fin = refs["fin"]
    for step, c in order:
        getattr(red, step)(c)


def all_reduce(g, bias, order=ORDER2):
    scratch = reduce_scratch()
    names = tuple(scratch)
    shape = (2, 3, 2, 4, 240, 640)
    out, bias = pl.pallas_call(
        functools.partial(ar_kernel, order, names),
        out_shape=(jax.ShapeDtypeStruct(shape, BF16), jax.ShapeDtypeStruct((8, 640), F32)),
        in_specs=[pl.BlockSpec(memory_space=pl.ANY), pl.BlockSpec(memory_space=pltpu.VMEM)],
        out_specs=(pl.BlockSpec(memory_space=pl.ANY), pl.BlockSpec(memory_space=pltpu.VMEM)),
        scratch_shapes=[pltpu.VMEM(shape, BF16)] + list(scratch.values()),
        compiler_params=pltpu.CompilerParams(collective_id=0, has_side_effects=True, vmem_limit_bytes=56 * 2**20),
        cost_estimate=pl.CostEstimate(flops=0, bytes_accessed=60 * 2**20, transcendentals=0),
    )(g.reshape(shape), bias)
    return out.reshape(2, 5760, 640), bias


MB = 2


sgld_step = 1.0


def passed_along(value, axis, steps):
    count = lax.axis_size(axis)
    pairs = [(source, (source + steps) % count) for source in range(count)]
    return lax.ppermute(value, axis, pairs)


def silu_slope(values):
    logistic = jax.nn.sigmoid(values)
    return logistic * (1.0 + values * (1.0 - logistic))


def windows(field_map, flipped):
    extent = field_map.shape[1]
    padded = jnp.pad(field_map, ((0, 0), (1, 1), (1, 1), (0, 0)))
    pieces = []
    for offset_row in range(3):
        for offset_col in range(3):
            top_row = 2 - offset_row if flipped else offset_row
            left_col = 2 - offset_col if flipped else offset_col
            pieces.append(padded[:, top_row : top_row + extent, left_col : left_col + extent, :])
    stacked = jnp.concatenate(pieces, axis=3)
    return stacked.reshape(-1, stacked.shape[3])


def product(left_side, right_side):
    return jnp.dot(left_side, right_side, preferred_element_type=jnp.float32)


def column_product(left_side, right_side):
    return lax.dot_general(
        left_side, right_side, (((0,), (0,)), ((), ())), preferred_element_type=jnp.float32
    )


def shape_back(flat_rows, like_map):
    return flat_rows.reshape(like_map.shape[:3] + (flat_rows.shape[1],))


def flip_kernel(kernel):
    channels = kernel.shape[3]
    return kernel.reshape(9, channels, channels).transpose(0, 2, 1).reshape(9 * channels, channels)


def region_of(groups, extent, inner_side):
    positions = jnp.arange(extent)
    inside = (positions[:, None] < inner_side) & (positions[None, :] < inner_side)
    kept_cells = (groups[:, None, None] == 1) | inside[None]
    return kept_cells.astype(jnp.float32)[..., None]


def distance_of(slot_index, total_slots, devices):
    return (2 * slot_index + 1) * devices // (2 * total_slots)


def second_conv_pass(inputs, region, cotangent, matrices):
    act_in = (jax.nn.silu(inputs) * region).astype(jnp.bfloat16)
    pre_one = shape_back(product(windows(act_in, False), matrices[0]), inputs) + matrices[1]
    act_mid = (jax.nn.silu(pre_one) * region).astype(jnp.bfloat16)
    cols_mid = windows(act_mid, False)
    pre_two = shape_back(product(cols_mid, matrices[2]), inputs) + matrices[3]
    output_map = ((inputs + pre_two) * region).astype(jnp.bfloat16)
    cot_low = (cotangent.astype(jnp.float32) * region).astype(jnp.bfloat16)
    flat_cot = cot_low.reshape(-1, cot_low.shape[3])
    kernel_part = column_product(cols_mid, flat_cot)
    bias_part = jnp.sum(flat_cot, axis=0, dtype=jnp.float32)
    back_mid = shape_back(product(windows(cot_low, True), matrices[5]), inputs)
    grad_one = (back_mid * silu_slope(pre_one) * region).astype(jnp.bfloat16)
    return (output_map, grad_one, kernel_part, bias_part)


def first_conv_pass(inputs, region, cotangent, grad_one, matrices):
    act_in = (jax.nn.silu(inputs) * region).astype(jnp.bfloat16)
    flat_grad = grad_one.reshape(-1, grad_one.shape[3])
    kernel_part = column_product(windows(act_in, False), flat_grad)
    bias_part = jnp.sum(flat_grad, axis=0, dtype=jnp.float32)
    back_in = shape_back(product(windows(grad_one, True), matrices[4]), inputs)
    cot_low = (cotangent.astype(jnp.float32) * region).astype(jnp.bfloat16)
    input_grad = cot_low.astype(jnp.float32) + back_in * region * silu_slope(inputs)
    return (input_grad, kernel_part, bias_part)


def zero_grads(channels):
    return (jnp.zeros((9 * channels, channels), jnp.float32), jnp.zeros((channels,), jnp.float32))


def chain_run(starts, probe_map, noises, matrices):
    back_mid = shape_back(product(windows(probe_map, True), matrices[5]), starts)
    probe_wide = probe_map.astype(jnp.float32)
    chain_state = starts
    for step_index in range(noises.shape[0]):
        act_in = jax.nn.silu(chain_state).astype(jnp.bfloat16)
        pre_one = (
            shape_back(product(windows(act_in, False), matrices[0]), chain_state) + matrices[1]
        )
        grad_one = (back_mid * silu_slope(pre_one)).astype(jnp.bfloat16)
        back_in = shape_back(product(windows(grad_one, True), matrices[4]), chain_state)
        chain_state = (
            chain_state
            + sgld_step * (probe_wide + back_in * silu_slope(chain_state))
            + noises[step_index].astype(jnp.float32)
        )
    return chain_state


def local(
    buffer_small,
    buffer_large,
    fetch_small,
    fetch_large,
    reinit_small,
    reinit_large,
    fresh_small,
    fresh_large,
    noise_small,
    noise_large,
    probe_small,
    probe_large,
    train_maps,
    train_group,
    train_cot,
    kernel_one,
    bias_one,
    kernel_two,
    bias_two,
):
    channels = kernel_one.shape[3]
    matrices = (
        kernel_one.reshape(9 * channels, channels),
        bias_one,
        kernel_two.reshape(9 * channels, channels),
        bias_two,
        flip_kernel(kernel_one),
        flip_kernel(kernel_two),
    )
    devices = lax.axis_size("dp")
    small_slots = fetch_small.shape[0]
    large_slots = fetch_large.shape[0]
    total_slots = small_slots + large_slots
    arrived_small = []
    for slot_index in range(small_slots):
        chosen = lax.dynamic_index_in_dim(buffer_small, fetch_small[slot_index], 0, keepdims=False)
        arrived_small.append(
            passed_along(chosen, "dp", distance_of(slot_index, total_slots, devices))
        )
    slot_index = 0
    chosen = lax.dynamic_index_in_dim(buffer_large, fetch_large[slot_index], 0, keepdims=False)
    arrived_large = [
        passed_along(chosen, "dp", distance_of(small_slots + slot_index, total_slots, devices))
    ]
    start_small = jnp.where(
        reinit_small[:, None, None, None] == 1,
        fresh_small.astype(jnp.float32),
        jnp.stack(arrived_small).astype(jnp.float32),
    )
    start_large = jnp.where(
        reinit_large[:, None, None, None] == 1,
        fresh_large.astype(jnp.float32),
        jnp.stack(arrived_large).astype(jnp.float32),
    )
    samples_small = chain_run(start_small, probe_small, noise_small, matrices).astype(jnp.bfloat16)
    samples_large = chain_run(start_large, probe_large, noise_large, matrices).astype(jnp.bfloat16)
    updated_small = buffer_small
    for slot_index in range(small_slots):
        returned = passed_along(
            samples_small[slot_index], "dp", devices - distance_of(slot_index, total_slots, devices)
        )
        updated_small = lax.dynamic_update_slice_in_dim(
            updated_small, returned[None], fetch_small[slot_index], 0
        )
    updated_large = buffer_large
    slot_index = 0
    returned = passed_along(
        samples_large[slot_index],
        "dp",
        devices - distance_of(small_slots + slot_index, total_slots, devices),
    )
    updated_large = lax.dynamic_update_slice_in_dim(
        updated_large, returned[None], fetch_large[slot_index], 0
    )
    micro_count = MB
    per_micro = train_maps.shape[0] // micro_count
    inner_side = buffer_small.shape[1]
    extent = train_maps.shape[1]
    kernel_one_sum, bias_one_sum = zero_grads(channels)
    kernel_two_sum, bias_two_sum = zero_grads(channels)
    outputs_list = []
    grads_list = []
    for micro_index in range(micro_count):
        first_map = micro_index * per_micro
        inputs = train_maps[first_map : first_map + per_micro].astype(jnp.float32)
        groups = train_group[first_map : first_map + per_micro]
        cotangent = train_cot[first_map : first_map + per_micro]
        region = region_of(groups, extent, inner_side)
        output_map, grad_one, kernel_part, bias_part = second_conv_pass(
            inputs, region, cotangent, matrices
        )
        kernel_two_sum = kernel_two_sum + kernel_part
        bias_two_sum = bias_two_sum + bias_part
        input_grad, kernel_part, bias_part = first_conv_pass(
            inputs, region, cotangent, grad_one, matrices
        )
        kernel_one_sum = kernel_one_sum + kernel_part
        bias_one_sum = bias_one_sum + bias_part
        outputs_list.append(output_map)
        grads_list.append(input_grad)
    partials = jnp.stack([kernel_two_sum, kernel_one_sum]).astype(BF16)
    bias_rows = jnp.pad(jnp.stack([bias_one_sum, bias_two_sum]), ((0, 6), (0, 0)))
    sums, bias_rows = all_reduce(partials, bias_rows)
    kernel_two_sum = sums[0].astype(F32)
    kernel_one_sum = sums[1].astype(F32)
    bias_one_sum, bias_two_sum = bias_rows[0], bias_rows[1]
    train_out = jnp.concatenate(outputs_list, axis=0)
    train_grad = jnp.concatenate(grads_list, axis=0)
    return (
        samples_small,
        samples_large,
        updated_small,
        updated_large,
        train_out,
        train_grad,
        kernel_one_sum.reshape(3, 3, channels, channels),
        bias_one_sum,
        kernel_two_sum.reshape(3, 3, channels, channels),
        bias_two_sum,
    )


def solution(mesh):
    in_specs = (
        P("dp", None, None, None),
        P("dp", None, None, None),
        P("dp"),
        P("dp"),
        P("dp"),
        P("dp"),
        P("dp", None, None, None),
        P("dp", None, None, None),
        P(None, "dp", None, None, None),
        P(None, "dp", None, None, None),
        P("dp", None, None, None),
        P("dp", None, None, None),
        P("dp", None, None, None),
        P("dp"),
        P("dp", None, None, None),
        P(),
        P(),
        P(),
        P(),
    )
    out_specs = (
        P("dp", None, None, None),
        P("dp", None, None, None),
        P("dp", None, None, None),
        P("dp", None, None, None),
        P("dp", None, None, None),
        P("dp", None, None, None),
        P(),
        P(),
        P(),
        P(),
    )
    return jax.shard_map(local, mesh=mesh, in_specs=in_specs, out_specs=out_specs, check_vma=False)
```

```python
import functools

import jax
import jax.numpy as jnp
from jax import lax
from jax.experimental import pallas as pl
from jax.experimental.pallas import tpu as pltpu
from jax.sharding import PartitionSpec as P

MESH = pl.DeviceIdType.MESH
F32 = jnp.float32
BF16 = jnp.bfloat16
STRIDES = (2, 8, 32)
KINDS = 48
SMALL_HOPS = (21, 64)
LARGE_HOP = 106


class Place:
    def __init__(self):
        me = lax.axis_index("dp")
        self.me = me
        self.core = lax.rem(me, 2)
        self.sib = me + 1 - 2 * self.core
        self.coord = [lax.rem(me // s, 4) for s in STRIDES]

    def near(self, axis, step):
        m = self.coord[axis]
        return self.me + (lax.rem(m + step, 4) - m) * STRIDES[axis]

    def hop(self, steps):
        return lax.rem(self.me + steps, 128)


class Copy:
    def __init__(self, src, dst, send, recv, dev):
        self.fields = dict(src_ref=src, dst_ref=dst, send_sem=send, recv_sem=recv, device_id=(dev,), device_id_type=MESH)

    def start(self):
        pltpu.make_async_remote_copy(**self.fields).start()

    def wait_send(self):
        pltpu.make_async_remote_copy(**self.fields).wait_send()

    def wait_recv(self):
        pltpu.make_async_remote_copy(**self.fields).wait_recv()


def rows_loop(total, step, body):
    def run(i, carry):
        body(pl.multiple_of(i * step, step))
        return carry

    lax.fori_loop(0, total // step, run, 0)


def peers(place):
    near = [place.near(a, s) for a in range(3) for s in (1, 2, 3)] + [place.sib]
    return near + [place.hop(s) for s in (21, 107, 64, 106, 22)]


def arrive(place):
    for device in peers(place):
        pl.semaphore_signal(pltpu.get_barrier_semaphore(), inc=1, device_id=(device,), device_id_type=MESH)


def all_arrived(place):
    pl.semaphore_wait(pltpu.get_barrier_semaphore(), len(peers(place)))


def sigmoid(v):
    return 1.0 / (1.0 + jnp.exp(-v))


def silu_slope(v):
    s = sigmoid(v)
    return s * (1.0 + v * (1.0 - s))


def rounded(v):
    return v.astype(BF16).astype(F32)


def dot(a, b):
    return jnp.dot(a, b, preferred_element_type=F32)


def dot_nt(a, b):
    return lax.dot_general(a, b, (((1,), (1,)), ((), ())), preferred_element_type=F32)


class Reduce:
    def __init__(self, refs):
        self.__dict__.update(refs)
        self.kinds = {}
        self.steps = (
            self.c0, self.s1, self.s1b, self.s2, self.s3, self.t3, self.t2, self.t1, self.t1b, self.t1c, self.t0,
            self.left, self.left_last, self.b0, self.b1,
        )

    def axes(self, p):
        return [p, (p + 1) % 3, (p + 2) % 3]

    def copy(self, c, p, kind, src, dst, dev):
        k = self.kinds.setdefault(kind, len(self.kinds))
        return Copy(src, dst, self.sends.at[c, p, k], self.recvs.at[c, p, k], dev)

    def span(self, core, block, start, size):
        return pl.ds(pl.multiple_of(core * 960 + block * 240 + start, 16), size)

    def d0(self, c, p):
        P = self.place
        far = pl.ds(pl.multiple_of((1 - P.core) * 960, 16), 960)
        return self.copy(c, p, "core", self.g.at[c, p, far], self.sib.at[c, p], P.sib)

    def d1(self, c, p):
        P = self.place
        ax = self.axes(p)[0]
        m = P.coord[ax]
        right, left, across = [lax.rem(m + d, 4) for d in (1, 3, 2)]
        dr, dl = P.near(ax, 1), P.near(ax, 3)
        first = lambda b: self.sib.at[c, p, self.span(0, b, 0, 128)]
        second = lambda b: self.sib.at[c, p, self.span(0, b, 128, 112)]
        h0, h1 = pl.ds(0, 128), pl.ds(128, 112)
        return dict(
            ar=self.copy(c, p, "1ar", first(across), self.r1o.at[c, p, 0], dr),
            al=self.copy(c, p, "1al", second(across), self.r1o.at[c, p, 1, pl.ds(0, 112)], dl),
            ra=self.copy(c, p, "1ra", second(right), self.r1.at[c, p, 0, h1], dr),
            la=self.copy(c, p, "1la", first(left), self.r1.at[c, p, 1, h0], dl),
            rb=self.copy(c, p, "1rb", first(right), self.r1.at[c, p, 0, h0], dr),
            lb=self.copy(c, p, "1lb", second(left), self.r1.at[c, p, 1, h1], dl),
        )

    def d2(self, c, p):
        P = self.place
        ax = self.axes(p)[1]
        return [
            self.copy(c, p, "2" + str(s), self.q1.at[c, p, lax.rem(P.coord[ax] + s, 4)], self.r2.at[c, p, s - 1], P.near(ax, s))
            for s in (2, 1, 3)
        ]

    def d3(self, c, p):
        P = self.place
        ax = self.axes(p)[2]
        return [
            self.copy(c, p, "3" + str(s), self.q2.at[c, p, lax.rem(P.coord[ax] + s, 4)], self.r3.at[c, p, s - 1], P.near(ax, s))
            for s in (2, 1, 3)
        ]

    def piece(self, p):
        second, third = self.axes(p)[1:]
        return pl.ds(pl.multiple_of(self.place.coord[second] * 64 + self.place.coord[third] * 16, 16), 16)

    def e3(self, c, p):
        third = self.axes(p)[2]
        mine = self.a2.at[c, p, self.piece(p)]
        return [self.copy(c, p, "e3" + str(s), mine, mine, self.place.near(third, s)) for s in (2, 1, 3)]

    def e2(self, c, p):
        second = self.axes(p)[1]
        mine = self.a2.at[c, p, pl.ds(pl.multiple_of(self.place.coord[second] * 64, 16), 64)]
        return [self.copy(c, p, "e2" + str(s), mine, mine, self.place.near(second, s)) for s in (2, 1, 3)]

    def e1(self, c, p):
        P = self.place
        ax = self.axes(p)[0]
        m = P.coord[ax]
        dr, dl = P.near(ax, 1), P.near(ax, 3)
        right, left, across = [lax.rem(m + d, 4) for d in (1, 3, 2)]
        block = lambda b: self.g.at[c, p, self.span(P.core, b, 0, 240)]
        first = lambda b: self.g.at[c, p, self.span(P.core, b, 0, 128)]
        second = lambda b: self.g.at[c, p, self.span(P.core, b, 128, 112)]
        src = self.a2.at[c, p, pl.ds(0, 240)]
        cp = functools.partial(self.copy, c, p)
        return dict(
            r=cp("e1r", src, block(m), dr),
            l=cp("e1l", src, block(m), dl),
            s=cp("e1s", src, block(m), P.sib),
            fr=cp("e1fr", first(left), first(left), dr),
            fl=cp("e1fl", second(right), second(right), dl),
            sr=cp("e1sr", block(right), block(right), P.sib),
            sl=cp("e1sl", block(left), block(left), P.sib),
            s0=cp("e1s0", first(across), first(across), P.sib),
            s1=cp("e1s1", second(across), second(across), P.sib),
        )

    def own(self, c, p):
        m = self.place.coord[self.axes(p)[0]]
        src = self.a2.at[c, p, pl.ds(0, 240)]
        return pltpu.make_async_copy(src, self.g.at[c, p, self.span(self.place.core, m, 0, 240)], self.local.at[c, p])

    def c0(self, c, p):
        self.d0(c, p).start()

    def s1(self, c, p):
        self.d0(c, p).wait_send()
        pl.semaphore_signal(self.free.at[c, p], inc=1, device_id=(self.place.sib,), device_id_type=MESH)
        self.d0(c, p).wait_recv()

        def add(r0):
            rows = pl.ds(r0, 48)
            mine = pl.ds(pl.multiple_of(self.place.core * 960 + r0, 16), 48)
            self.sib[c, p, rows, :] = (self.sib[c, p, rows, :].astype(F32) + self.g[c, p, mine, :].astype(F32)).astype(BF16)

        rows_loop(960, 48, add)
        d = self.d1(c, p)
        for k in ("ar", "al", "ra", "la"):
            d[k].start()

    def s1b(self, c, p):
        d = self.d1(c, p)
        m = self.place.coord[self.axes(p)[0]]
        right, left = lax.rem(m + 1, 4), lax.rem(m + 3, 4)

        def add(block, start, count, slot):
            def some(r0):
                to = pl.ds(pl.multiple_of(block * 240 + start + r0, 16), 16)
                part = self.r1o[c, p, slot, pl.ds(r0, 16), :].astype(F32)
                self.sib[c, p, to, :] = (self.sib[c, p, to, :].astype(F32) + part).astype(BF16)

            rows_loop(count, 16, some)

        d["ar"].wait_recv()
        add(right, 0, 128, 0)
        d["rb"].start()
        d["al"].wait_recv()
        add(left, 128, 112, 1)
        d["lb"].start()

    def s2(self, c, p):
        d = self.d1(c, p)
        m = self.place.coord[self.axes(p)[0]]
        for k in ("ra", "la", "rb", "lb"):
            d[k].wait_recv()

        def add(r0):
            rows = pl.ds(r0, 16)
            mine = pl.ds(pl.multiple_of(m * 240 + r0, 16), 16)
            total = self.sib[c, p, mine, :].astype(F32) + self.r1[c, p, 0, rows, :].astype(F32)
            total = total + self.r1[c, p, 1, rows, :].astype(F32)
            b = r0 // 64
            self.q1[c, p, b, pl.ds(pl.multiple_of(r0 - b * 64, 16), 16), :] = total.astype(BF16)

        rows_loop(240, 16, add)
        self.q1[c, p, 3, 48:64, :] = jnp.zeros((16, 640), BF16)
        for k in self.d2(c, p):
            k.start()

    def level2(self, c, p, b):
        m = self.place.coord[self.axes(p)[1]]
        rows = pl.ds(pl.multiple_of(b * 16, 16), 16)
        total = self.q1[c, p, m, rows, :].astype(F32)
        for s in range(3):
            total = total + self.r2[c, p, s, rows, :].astype(F32)
        return total

    def s3(self, c, p):
        for k in self.d2(c, p):
            k.wait_recv()

        def add(b, carry):
            self.q2[c, p, b] = self.level2(c, p, b).astype(BF16)
            return carry

        lax.fori_loop(0, 4, add, 0)
        for k in self.d3(c, p):
            k.start()

    def t3(self, c, p):
        for k in self.d3(c, p):
            k.wait_recv()
        total = self.level2(c, p, self.place.coord[self.axes(p)[2]])
        for s in range(3):
            total = total + self.r3[c, p, s].astype(F32)
        self.a2[c, p, self.piece(p), :] = total.astype(BF16)
        for k in self.e3(c, p):
            k.start()

    def t2(self, c, p):
        for k in self.e3(c, p):
            k.wait_recv()
        for k in self.e2(c, p):
            k.start()

    def t1(self, c, p):
        for k in self.e2(c, p):
            k.wait_recv()
        e = self.e1(c, p)
        e["r"].start()
        e["l"].start()
        pl.semaphore_wait(self.free.at[c, p], 1)
        e["s"].start()
        self.own(c, p).start()

    def t1b(self, c, p):
        e = self.e1(c, p)
        e["r"].wait_recv()
        e["fr"].start()
        e["sl"].start()
        e["l"].wait_recv()
        e["fl"].start()
        e["sr"].start()

    def t1c(self, c, p):
        e = self.e1(c, p)
        e["fr"].wait_recv()
        e["s0"].start()
        e["fl"].wait_recv()
        e["s1"].start()

    def t0(self, c, p):
        e = self.e1(c, p)
        for k in ("s", "sr", "sl", "s0", "s1"):
            e[k].wait_recv()
        self.own(c, p).wait()

    def bias_copies(self, level):
        P = self.place
        if level == 0:
            peers = [(0, P.sib, P.core)]
        else:
            peers = [(s, P.near(level - 1, s), P.coord[level - 1]) for s in (1, 2, 3)]
        return [
            self.copy(0, 0, "b%d%d" % (level, s), self.bias.at[level, slot], self.bias.at[level, slot], dev)
            for s, dev, slot in peers
        ]

    def b0(self, c, p):
        level = 3 * c + p
        for k in self.bias_copies(level):
            k.start()

    def b1(self, c, p):
        level = 3 * c + p
        for k in self.bias_copies(level):
            k.wait_recv()
        total = self.bias[level, 0] + self.bias[level, 1]
        if level:
            total = total + self.bias[level, 2] + self.bias[level, 3]
        if level < 3:
            self.bias[level + 1, self.place.coord[level]] = total
            self.b0((level + 1) // 3, (level + 1) % 3)
        else:
            self.bias_out[...] = total

    def left(self, c, p):
        for k in list(self.d1(c, p).values()) + self.d2(c, p) + self.d3(c, p) + self.e3(c, p) + self.e2(c, p):
            k.wait_send()

    def left_last(self, c, p):
        for k in self.e1(c, p).values():
            k.wait_send()

    def finish(self):
        for p in range(3):
            self.left_last(1, p)
        for level in range(4):
            for k in self.bias_copies(level):
                k.wait_send()


def reduce_scratch():
    v = lambda *s: pltpu.VMEM((2, 3) + s, BF16)
    sems = pltpu.SemaphoreType.DMA((2, 3, KINDS))
    return dict(
        sib=v(960, 640),
        r1=v(2, 240, 640),
        r1o=v(2, 128, 640),
        r2=v(3, 64, 640),
        r3=v(3, 16, 640),
        q1=v(4, 64, 640),
        q2=v(4, 16, 640),
        a2=v(256, 640),
        bias=pltpu.VMEM((4, 4, 8, 640), F32),
        sends=sems,
        recvs=sems,
        local=pltpu.SemaphoreType.DMA((2, 3)),
        free=pltpu.SemaphoreType.REGULAR((2, 3)),
    )


class Block:
    def __init__(self, refs):
        self.__dict__.update(refs)

    def load(self, which, r):
        src = (self.kernel_one, self.kernel_two)[which].at[r]
        return pltpu.make_async_copy(src, self.taps.at[r], self.tap_sems.at[r])

    def wait_taps(self, r):
        self.load(0, r).wait()

    def fetch(self, name):
        k = self.inputs.index(name)
        return pltpu.make_async_copy(getattr(self, name), getattr(self, name + "_v"), self.in_sems.at[k])

    def begin(self):
        zeros = jnp.zeros((16, 640), F32)
        self.borders()
        self.xp[0:8, :] = zeros[:8]
        self.xp[584:592, :] = zeros[:8]
        for start in (0, 80, 160):
            self.xs[start : start + 16, :] = zeros[:16]
        self.xl[0:16, :] = zeros[:16]
        self.xl[160:176, :] = zeros[:16]

        def edges(base, count, column):
            n = lax.broadcasted_iota(jnp.int32, (count, 128), 0)
            j, last = column(n)
            self.edge[0, base : base + count, :] = jnp.where(j > 0, 1.0, 0.0)
            self.edge[1, base : base + count, :] = jnp.where(j < last, 1.0, 0.0)

        def twelfth(n):
            return (n * 43691) >> 19

        def wide(n):
            return n - 12 * twelfth(n), 11

        edges(0, 576, lambda n: wide(n >> 2))
        edges(576, 128, lambda n: (n & 7, 7))
        edges(704, 144, wide)
        n = lax.broadcasted_iota(jnp.int32, (576, 128), 0)
        cell = n >> 2
        i = twelfth(cell)
        j = cell - 12 * i
        keep = jnp.where((i < 8) & (j < 8), 1.0, 0.0)
        for m in range(4):
            group = jnp.where(self.group[m] == 1, 1.0, 0.0)
            keep = jnp.maximum(keep, jnp.where((n & 3) == m, group, 0.0))
        self.region[...] = keep

    def borders(self):
        self.cols[0:48, :] = jnp.zeros((48, 1920), BF16)
        self.cols[624:672, :] = jnp.zeros((48, 1920), BF16)

    def train_cols(self, sign):
        for q in range(3):
            dj = sign * (q - 1)
            v = self.xp[pl.ds(8 + dj * 4, 576), :]
            if dj:
                v = v * self.edge[(dj + 1) // 2, 0:576, 0:1]
            self.cols[48:624, q * 640 : (q + 1) * 640] = v.astype(BF16)

    def chain_cols(self, sign):
        for r in range(3):
            self.chain_row(r, sign, self.cols.at[pl.ds(272 * r, 272)])

    def chain_row(self, r, sign, cols):
        for q in range(3):
            dj = sign * (q - 1)
            to = pl.ds(q * 640, 640)
            for m in range(2):
                v = self.xs[pl.ds(16 + 80 * m + sign * (r - 1) * 8 + dj, 64), :]
                if dj:
                    v = v * self.edge[(dj + 1) // 2, 576 + 64 * m : 640 + 64 * m, 0:1]
                cols[64 * m : 64 * m + 64, to] = v.astype(BF16)
            v = self.xl[pl.ds(16 + sign * (r - 1) * 12 + dj, 144), :]
            if dj:
                v = v * self.edge[(dj + 1) // 2, 704:848, 0:1]
            cols[128:272, to] = v.astype(BF16)

    def clear(self):
        self.acc[...] = jnp.zeros((576, 640), F32)

    def product(self, r, rows, back, cols):
        taps = self.taps.at[r]
        if back:
            total = None
            for q in range(3):
                cut = pl.ds(q * 640, 640)
                part = dot_nt(cols[:, cut], taps[cut, :])
                total = part if total is None else total + part
        else:
            total = dot(cols[...], taps[...])
        self.acc[0:rows, :] += total

    def train_side(self, r, sign):
        return self.cols.at[pl.ds(pl.multiple_of(48 + sign * (r - 1) * 48, 16), 576)]

    def train_conv(self, back, wait, then, r):
        if wait:
            self.wait_taps(r)
        self.product(r, 576, back, self.train_side(r, -1 if back else 1))
        if then is not None:
            self.load(then, r).start()

    def chain_conv(self, back, wait, then, r):
        if wait is not None:

            @pl.when(wait)
            def _():
                self.wait_taps(r)

        self.product(r, 272, back, self.cols.at[pl.ds(pl.multiple_of(272 * r, 16), 272)])
        if then is not None:
            self.load(then, r).start()

    def train_wgrad(self, chunk, r):
        side = self.train_side(r, -1)
        for start, size in ((0, 768), (768, 768), (1536, 384)):
            part = dot(self.turned[...], side[:, start : start + size]).astype(BF16)
            for q in range(3):
                low, high = max(start, q * 640), min(start + size, q * 640 + 640)
                if low < high:
                    self.g[chunk, r, q * 640 : q * 640 + 640, low - q * 640 : high - q * 640] = part[:, low - start : high - start]

    def map_rows(self, ref, r0):
        return ref[pl.ds(r0 // 4, 12)].astype(F32).reshape(48, 640)

    def train_start(self):
        self.fetch("maps").wait()
        def some(r0):
            rows = pl.ds(r0, 48)
            v = self.map_rows(self.maps_v, r0)
            a = (v * sigmoid(v) * self.region[rows, 0:1]).astype(BF16)
            self.low_in[rows, :] = a
            self.xp[pl.ds(pl.multiple_of(r0 + 8, 8), 48), :] = a.astype(F32)

        rows_loop(576, 48, some)
        self.train_cols(1)
        self.clear()

    def train_middle(self):
        self.fetch("cot").wait()
        self.sums[...] = jnp.zeros((8, 640), F32)

        def some(r0):
            rows = pl.ds(r0, 48)
            v = self.acc[rows, :] + self.bias_one[...].reshape(1, 640)
            keep = self.region[rows, 0:1]
            self.low_mid[rows, :] = (v * sigmoid(v) * keep).astype(BF16)
            self.pre_one[rows, :] = silu_slope(v) * keep
            c = self.map_rows(self.cot_v, r0) * keep
            self.xp[pl.ds(pl.multiple_of(r0 + 8, 8), 48), :] = c
            self.sums[1:2, :] += jnp.sum(c, axis=0, keepdims=True)

        rows_loop(576, 48, some)
        self.turned[...] = self.low_mid[...].T
        self.train_cols(-1)
        self.clear()

    def train_back(self):
        def some(r0):
            rows = pl.ds(r0, 48)
            v = rounded(self.acc[rows, :] * self.pre_one[rows, :])
            self.xp[pl.ds(pl.multiple_of(r0 + 8, 8), 48), :] = v
            self.sums[0:1, :] += jnp.sum(v, axis=0, keepdims=True)

        rows_loop(576, 48, some)
        self.turned[...] = self.low_in[...].T
        self.bias[0, self.place.core] = self.sums[...]
        self.train_cols(-1)

    def put_xp(self, low):
        def some(r0):
            rows = pl.ds(r0, 48)
            self.xp[pl.ds(pl.multiple_of(r0 + 8, 8), 48), :] = low[rows, :].astype(F32)

        rows_loop(576, 48, some)
        self.train_cols(1)
        self.clear()

    def train_grad_end(self):
        def some(r0):
            rows = pl.ds(r0, 48)
            keep = self.region[rows, 0:1]
            slope = silu_slope(self.map_rows(self.maps_v, r0)) * keep
            self.acc[rows, :] = self.map_rows(self.cot_v, r0) * keep + self.acc[rows, :] * slope

        rows_loop(576, 48, some)
        self.grad[...] = self.acc[...].reshape(144, 4, 640)

    def train_out_end(self):
        def some(r0):
            rows = pl.ds(r0, 48)
            v = self.map_rows(self.maps_v, r0) + (self.acc[rows, :] + self.bias_two[...].reshape(1, 640))
            self.acc[rows, :] = v * self.region[rows, 0:1]

        rows_loop(576, 48, some)
        self.out[...] = self.acc[...].astype(BF16).reshape(144, 4, 640)

    def chain_peers(self):
        P = self.place
        pairs = []
        for s in range(2):
            cut = pl.ds(8 * s, 8)
            pairs.append((s, self.chosen_small.at[cut], self.arrived_small.at[cut], self.samples_small.at[cut], self.ret_small.at[cut], SMALL_HOPS[s]))
        pairs.append((2, self.chosen_large, self.arrived_large, self.samples_large, self.ret_large, LARGE_HOP))
        there = [Copy(a, b, self.go_sems.at[0, k], self.go_sems.at[1, k], P.hop(h)) for k, a, b, _, _, h in pairs]
        back = [Copy(a, b, self.go_sems.at[2, k], self.go_sems.at[3, k], P.hop(128 - h)) for k, _, _, a, b, h in pairs]
        return there, back

    def buffers(self):
        return [
            pltpu.make_async_copy(self.buffer_small, self.g.at[1, 0, pl.ds(0, 1024)], self.buffer_sems.at[0]),
            pltpu.make_async_copy(self.buffer_large, self.g.at[1, 1, pl.ds(0, 1152)], self.buffer_sems.at[1]),
        ]

    def chain_send(self):
        all_arrived(self.place)
        for k in self.buffers():
            k.wait()
        n = lax.broadcasted_iota(jnp.int32, (128, 1024), 0)
        at = lax.broadcasted_iota(jnp.int32, (128, 1024), 1)
        start = jnp.where(n < 64, self.fetch_small[0], self.fetch_small[1]) * 64
        pick = jnp.where(at == start + (n & 63), 1.0, 0.0).astype(BF16)
        rows = dot(pick, self.g[1, 0, 0:1024, :]).astype(BF16)
        self.chosen_small[...] = rows.reshape(16, 8, 640)
        n = lax.broadcasted_iota(jnp.int32, (144, 1152), 0)
        at = lax.broadcasted_iota(jnp.int32, (144, 1152), 1)
        pick = jnp.where(at == n * 8 + self.fetch_large[0], 1.0, 0.0).astype(BF16)
        rows = dot(pick, self.g[1, 1, 0:1152, :]).astype(BF16)
        for i in range(12):
            self.chosen_large[i] = rows[12 * i : 12 * i + 12]
        for k in self.chain_peers()[0]:
            k.start()

    def flat_small(self, ref):
        return ref.astype(F32).reshape(128, 640)

    def spread(self, value):
        for m in range(2):

            def small(r0, m=m):
                self.xs[pl.ds(pl.multiple_of(16 + 80 * m + r0, 8), 16), :] = value(pl.multiple_of(64 * m + r0, 16))

            rows_loop(64, 16, small)

        def large(r0):
            self.xl[pl.ds(pl.multiple_of(16 + r0, 8), 16), :] = value(pl.multiple_of(128 + r0, 16))

        rows_loop(144, 16, large)

    def chain_start(self):
        for name in ("probe_small", "probe_large"):
            self.fetch(name).wait()
        self.probe[0:128, :] = self.flat_small(self.probe_small_v[...])
        for i in range(12):
            self.probe[128 + 12 * i : 140 + 12 * i, :] = self.probe_large_v[i].astype(F32)
        self.spread(lambda r0: self.probe[pl.ds(r0, 16), :])
        self.chain_cols(-1)
        self.clear()

    def chain_state(self):
        for name in ("fresh_small", "fresh_large", "noise_small", "noise_large"):
            self.fetch(name).wait()
        for k in self.chain_peers()[0]:
            k.wait_recv()
        for s in range(2):
            fresh = jnp.where(self.reinit_small[s] == 1, 1.0, 0.0)
            cut = slice(8 * s, 8 * s + 8)
            v = self.fresh_small_v[cut].astype(F32) * fresh + self.arrived_small[cut].astype(F32) * (1.0 - fresh)
            self.state[64 * s : 64 * s + 64, :] = v.reshape(64, 640)
        fresh = jnp.where(self.reinit_large[0] == 1, 1.0, 0.0)
        for i in range(12):
            v = self.fresh_large_v[i].astype(F32) * fresh + self.arrived_large[i].astype(F32) * (1.0 - fresh)
            self.state[128 + 12 * i : 140 + 12 * i, :] = v

    def chain_kept(self):
        self.slope_in[...] = self.acc[0:272, :]

    def chain_act(self):
        def value(r0):
            v = self.state[pl.ds(r0, 16), :]
            return rounded(v * sigmoid(v))

        self.spread(value)
        self.chain_cols(1)
        self.clear()

    def chain_mid(self):
        def value(r0):
            rows = pl.ds(r0, 16)
            v = self.acc[rows, :] + self.bias_one[...].reshape(1, 640)
            return rounded(silu_slope(v) * self.slope_in[rows, :])

        self.spread(value)
        self.chain_cols(-1)
        self.clear()

    def chain_step(self, t):
        late = jnp.where(t == 1, 1.0, 0.0)
        early = 1.0 - late

        def small(r0):
            rows = pl.ds(r0, 16)
            v = self.state[rows, :]
            noise = self.noise_small_v[t, pl.ds(r0 // 8, 2)].astype(F32).reshape(16, 640)
            self.state[rows, :] = v + (self.probe[rows, :] + silu_slope(v) * self.acc[rows, :]) + noise

        rows_loop(128, 16, small)

        def large(r0):
            rows = pl.ds(pl.multiple_of(128 + r0, 16), 16)
            v = self.state[rows, :]
            noise = self.noise_large_v[pl.ds(r0, 16)].astype(F32)
            noise = noise[:, 0, :] * early + noise[:, 1, :] * late
            self.state[rows, :] = v + (self.probe[rows, :] + silu_slope(v) * self.acc[rows, :]) + noise

        rows_loop(144, 16, large)

    def chain_end(self):
        self.samples_small[...] = self.state[0:128, :].astype(BF16).reshape(16, 8, 640)
        for i in range(12):
            self.samples_large[i] = self.state[128 + 12 * i : 140 + 12 * i, :].astype(BF16)
        for k in self.chain_peers()[1]:
            k.start()
        self.borders()
        self.train_cols(-1)
        self.clear()

    def finish(self):
        there, back = self.chain_peers()
        for k in back:
            k.wait_recv()
        for k in there + back:
            k.wait_send()


INPUTS = (
    "maps", "cot", "probe_small", "probe_large", "fresh_small", "fresh_large", "noise_small", "noise_large",
)
OUTPUTS = ("samples_small", "samples_large", "out", "grad")
INPUT_SHAPES = (
    (144, 4, 640), (144, 4, 640), (16, 8, 640), (12, 12, 640), (16, 8, 640), (12, 12, 640), (2, 16, 8, 640), (144, 2, 640),
)


def block_scratch():
    f = lambda *s: pltpu.VMEM(s, F32)
    b = lambda *s: pltpu.VMEM(s, BF16)
    dma = pltpu.SemaphoreType.DMA
    found = {name + "_v": b(*shape) for name, shape in zip(INPUTS, INPUT_SHAPES)}
    found.update(
        taps=b(3, 1920, 640),
        cols=b(816, 1920),
        xp=f(592, 640),
        xs=f(176, 640),
        xl=f(176, 640),
        acc=f(576, 640),
        pre_one=f(576, 640),
        low_in=b(576, 640),
        low_mid=b(576, 640),
        turned=b(640, 576),
        edge=f(2, 848, 128),
        region=f(576, 128),
        sums=f(8, 640),
        probe=f(272, 640),
        state=f(272, 640),
        slope_in=f(272, 640),
        arrived_small=b(16, 8, 640),
        arrived_large=b(12, 12, 640),
        chosen_small=b(16, 8, 640),
        chosen_large=b(12, 12, 640),
        tap_sems=dma((3,)),
        in_sems=dma((len(INPUTS),)),
        buffer_sems=dma((2,)),
        go_sems=dma((4, 3)),
    )
    return found


class Loop:
    def __init__(self, count, body):
        self.count, self.body = count, body


def length(items):
    return sum(i.count * length(i.body(None)) if isinstance(i, Loop) else 1 for i in items)


def schedule(block):
    part = functools.partial

    def conv(back, wait=False, then=None):
        return Loop(3, lambda r: [part(block.train_conv, back, wait, then, r)])

    def chain(back, wait=None, then=None):
        return Loop(3, lambda r: [part(block.chain_conv, back, wait, then, r)])

    def wgrad(chunk):
        return Loop(3, lambda r: [part(block.train_wgrad, chunk, r)])

    def chain_turn(t):
        first = None if t is None else t == 0
        return [block.chain_act, chain(False, wait=first), block.chain_mid, chain(True), part(block.chain_step, t)]

    return [
        block.train_start,
        conv(False, wait=True, then=1),
        block.chain_send,
        block.train_middle,
        wgrad(0),
        conv(True, wait=True),
        block.train_back,
        wgrad(1),
        block.chain_start,
        chain(True, then=0),
        block.chain_kept,
        block.chain_state,
        Loop(2, chain_turn),
        block.chain_end,
        conv(True, then=1),
        block.train_grad_end,
        part(block.put_xp, block.low_mid),
        conv(False, wait=True),
        block.train_out_end,
    ]


def play(items, places, tick):
    done = 0
    for item in items:
        if isinstance(item, Loop):
            size = length(item.body(None))

            def turn(i, carry, item=item, size=size, done=done):
                inner = []
                for condition, base in places:
                    for k in range(item.count):
                        now = i == k
                        inner.append((now if condition is None else condition & now, base + done + k * size))
                play(item.body(i), inner, tick)
                return carry

            lax.fori_loop(0, item.count, turn, 0)
            done += item.count * size
        else:
            item()
            for condition, base in places:
                tick(condition, base + done)
            done += 1


TICKS = {
    6: (0,),
    8: (6, 1,),
    9: (2,),
    10: (7,),
    11: (12, 8,),
    12: (78,),
    13: (13, 3,),
    14: (4, 18, 14, 9,),
    15: (5, 19, 10, 84,),
    17: (11, 20,),
    19: (15, 85,),
    21: (16, 25,),
    22: (24,),
    23: (17, 86,),
    24: (26,),
    25: (21, 30, 22,),
    26: (31,),
    27: (32, 23, 87,),
    28: (36,),
    29: (27,),
    30: (28, 38,),
    32: (29, 33,),
    33: (34, 37, 42,),
    34: (35, 39,),
    35: (40,),
    37: (44, 43, 41,),
    39: (45, 46,),
    41: (48, 47,),
    42: (49,),
    45: (50, 51,),
    46: (52, 53, 54,),
    47: (56, 55, 57,),
    48: (62, 58, 60, 59,),
    49: (66, 67, 68, 69, 70, 71, 72, 73, 74, 63, 64, 61, 65,),
}

B_INPUTS = INPUTS + (
    "buffer_small", "buffer_large", "kernel_one", "kernel_two",
    "group", "reinit_small", "reinit_large", "fetch_small", "fetch_large", "bias_one", "bias_two",
)
B_OUTPUTS = ("g",) + OUTPUTS + ("ret_small", "ret_large", "bias_out")


def block_kernel(names, *given):
    refs = dict(zip(names, given))
    refs.update(place=Place(), inputs=INPUTS)
    block, reduce = Block(refs), Reduce(refs)
    arrive(block.place)
    block.fetch("maps").start()
    for r in range(3):
        block.load(0, r).start()
    for k in block.buffers():
        k.start()
    for name in INPUTS[1:]:
        block.fetch(name).start()
    block.begin()

    def tick(condition, n):
        def run():
            for code in TICKS.get(n, ()):
                reduce.steps[code // 6](code // 3 % 2, code % 3)

        if condition is None:
            run()
        elif n in TICKS:
            pl.when(condition)(run)

    play(schedule(block), [(None, 0)], tick)
    block.finish()
    reduce.finish()


ANYWHERE = pl.BlockSpec(memory_space=pl.ANY)
SCALARS = pl.BlockSpec(memory_space=pltpu.SMEM)
INSIDE = pl.BlockSpec(memory_space=pltpu.VMEM)


def run_block(*args):
    scratch = reduce_scratch()
    scratch.update(block_scratch())
    names = B_INPUTS + B_OUTPUTS + tuple(scratch)
    held = [pltpu.with_memory_space_constraint(a, pltpu.HBM) if k < 12 else a for k, a in enumerate(args)]
    return pl.pallas_call(
        functools.partial(block_kernel, names),
        out_shape=(
            pltpu.VMEM((2, 3, 1920, 640), BF16),
            pltpu.VMEM((16, 8, 640), BF16),
            pltpu.VMEM((12, 12, 640), BF16),
            pltpu.VMEM((144, 4, 640), BF16),
            pltpu.VMEM((144, 4, 640), F32),
            pltpu.VMEM((16, 8, 640), BF16),
            pltpu.VMEM((12, 12, 640), BF16),
            pltpu.VMEM((8, 640), F32),
        ),
        in_specs=[ANYWHERE] * 12 + [SCALARS] * 5 + [INSIDE] * 2,
        out_specs=(INSIDE,) * 8,
        scratch_shapes=list(scratch.values()),
        compiler_params=pltpu.CompilerParams(collective_id=0, has_side_effects=True, vmem_limit_bytes=46 * 2**20),
        cost_estimate=pl.CostEstimate(flops=36 * 10**9, bytes_accessed=80 * 2**20, transcendentals=0),
    )(*held)


END_INPUTS = (
    "g", "samples_small_in", "samples_large_in", "out_in", "grad_in", "ret_small", "ret_large", "bias",
    "buffer_small", "buffer_large", "fetch_small", "fetch_large",
)
END_OUTPUTS = (
    "kernel_one", "kernel_two", "samples_small", "samples_large", "out", "grad", "new_small", "new_large", "bias_one", "bias_two",
)
END_SCRATCH = ("wide", "small", "large", "wide_sems", "sems")
PASSED = ("out", "grad", "samples_small", "samples_large")
CUT = 480
SLOTS = 4


def end_kernel(*given):
    r = dict(zip(END_INPUTS + END_OUTPUTS + END_SCRATCH, given))
    sems = r["sems"]
    small = pltpu.make_async_copy(r["buffer_small"], r["small"], sems.at[4])
    large = pltpu.make_async_copy(r["buffer_large"], r["large"], sems.at[5])
    small.start()
    large.start()
    passed = [pltpu.make_async_copy(r[n + "_in"], r[n], sems.at[k]) for k, n in enumerate(PASSED)]
    per_part = 1920 // CUT
    pending = []
    for n in range(6 * per_part):
        c, part, block = n // (3 * per_part), n // per_part % 3, n % per_part
        slot = n % SLOTS
        target = r["kernel_one"] if c else r["kernel_two"]
        copy = pltpu.make_async_copy(
            r["wide"].at[slot], target.at[pl.ds(part * 1920 + block * CUT, CUT)], r["wide_sems"].at[slot]
        )
        if n >= SLOTS:
            pending[n - SLOTS].wait()

        def some(r0):
            rows = pl.ds(pl.multiple_of(block * CUT + r0, 16), 96)
            r["wide"][slot, pl.ds(r0, 96), :] = r["g"][c, part, rows, :].astype(F32)

        rows_loop(CUT, 96, some)
        copy.start()
        pending.append(copy)
        if n == 0:
            for k in passed:
                k.start()
            r["bias_one"][...] = r["bias"][0, :]
            r["bias_two"][...] = r["bias"][1, :]
        if n == per_part:
            small.wait()
            for s in range(2):
                r["small"][r["fetch_small"][s]] = r["ret_small"][8 * s : 8 * s + 8]
            small = pltpu.make_async_copy(r["small"], r["new_small"], sems.at[4])
            small.start()
        if n == 2 * per_part:
            large.wait()
            chosen = lax.broadcasted_iota(jnp.int32, (12, 8, 640), 1) == r["fetch_large"][0]
            for i in range(12):
                cut = slice(12 * i, 12 * i + 12)
                new = jnp.broadcast_to(r["ret_large"][i].astype(F32)[:, None, :], (12, 8, 640))
                r["large"][cut] = jnp.where(chosen, new, r["large"][cut].astype(F32)).astype(BF16)
            large = pltpu.make_async_copy(r["large"], r["new_large"], sems.at[5])
            large.start()
    for k in pending[-SLOTS:] + passed + [small, large]:
        k.wait()


def run_end(*args):
    shape = pltpu.HBM
    held = [pltpu.with_memory_space_constraint(a, pltpu.HBM) if k in (8, 9) else a for k, a in enumerate(args)]
    return pl.pallas_call(
        end_kernel,
        out_shape=(
            shape((5760, 640), F32),
            shape((5760, 640), F32),
            shape((16, 8, 640), BF16),
            shape((12, 12, 640), BF16),
            shape((144, 4, 640), BF16),
            shape((144, 4, 640), F32),
            shape((16, 8, 8, 640), BF16),
            shape((144, 8, 640), BF16),
            jax.ShapeDtypeStruct((640,), F32),
            jax.ShapeDtypeStruct((640,), F32),
        ),
        in_specs=[INSIDE] * 8 + [ANYWHERE] * 2 + [SCALARS] * 2,
        out_specs=(ANYWHERE,) * 8 + (INSIDE,) * 2,
        scratch_shapes=[
            pltpu.VMEM((SLOTS, CUT, 640), F32),
            pltpu.VMEM((16, 8, 8, 640), BF16),
            pltpu.VMEM((144, 8, 640), BF16),
            pltpu.SemaphoreType.DMA((SLOTS,)),
            pltpu.SemaphoreType.DMA((6,)),
        ],
        compiler_params=pltpu.CompilerParams(vmem_limit_bytes=16 * 2**20),
    )(*held)


def map_minor(v):
    return v.transpose(1, 2, 0, 3).reshape(144, v.shape[0], 640)


def map_major(v):
    return v.reshape(12, 12, v.shape[1], 640).transpose(2, 0, 1, 3)


def local(
    buffer_small,
    buffer_large,
    fetch_small,
    fetch_large,
    reinit_small,
    reinit_large,
    fresh_small,
    fresh_large,
    noise_small,
    noise_large,
    probe_small,
    probe_large,
    train_maps,
    train_group,
    train_cot,
    kernel_one,
    bias_one,
    kernel_two,
    bias_two,
):
    g, samples_small, samples_large, out, grad, ret_small, ret_large, bias = run_block(
        map_minor(train_maps),
        map_minor(train_cot),
        probe_small.reshape(16, 8, 640),
        probe_large.reshape(12, 12, 640),
        fresh_small.reshape(16, 8, 640),
        fresh_large.reshape(12, 12, 640),
        noise_small.reshape(2, 16, 8, 640),
        noise_large.transpose(1, 2, 3, 0, 4).reshape(144, 2, 640),
        buffer_small.reshape(1024, 640),
        map_minor(buffer_large).reshape(1152, 640),
        kernel_one.reshape(3, 1920, 640),
        kernel_two.reshape(3, 1920, 640),
        train_group,
        reinit_small,
        reinit_large,
        fetch_small,
        fetch_large,
        bias_one,
        bias_two,
    )
    sums = run_end(
        g, samples_small, samples_large, out, grad, ret_small, ret_large, bias,
        buffer_small, map_minor(buffer_large), fetch_small, fetch_large,
    )
    sum_one, sum_two, samples_small, samples_large, out, grad, new_small, new_large, bias_sum_one, bias_sum_two = sums
    return (
        samples_small.reshape(2, 8, 8, 640),
        samples_large.reshape(1, 12, 12, 640),
        new_small,
        map_major(new_large),
        map_major(out),
        map_major(grad),
        sum_one.reshape(3, 3, 640, 640),
        bias_sum_one,
        sum_two.reshape(3, 3, 640, 640),
        bias_sum_two,
    )


def solution(mesh):
    in_specs = (
        P("dp", None, None, None),
        P("dp", None, None, None),
        P("dp"),
        P("dp"),
        P("dp"),
        P("dp"),
        P("dp", None, None, None),
        P("dp", None, None, None),
        P(None, "dp", None, None, None),
        P(None, "dp", None, None, None),
        P("dp", None, None, None),
        P("dp", None, None, None),
        P("dp", None, None, None),
        P("dp"),
        P("dp", None, None, None),
        P(),
        P(),
        P(),
        P(),
    )
    out_specs = (
        P("dp", None, None, None),
        P("dp", None, None, None),
        P("dp", None, None, None),
        P("dp", None, None, None),
        P("dp", None, None, None),
        P("dp", None, None, None),
        P(),
        P(),
        P(),
        P(),
    )
    return jax.shard_map(local, mesh=mesh, in_specs=in_specs, out_specs=out_specs, check_vma=False)
```

```python
import functools

import jax
import jax.numpy as jnp
from jax import lax
from jax.experimental import pallas as pl
from jax.experimental.pallas import tpu as pltpu
from jax.sharding import PartitionSpec as P

MESH = pl.DeviceIdType.MESH
F32 = jnp.float32
BF16 = jnp.bfloat16
STRIDES = (2, 8, 32)
KINDS = 48
SMALL_HOPS = (21, 64)
LARGE_HOP = 106


class Place:
    def __init__(self):
        me = lax.axis_index("dp")
        self.me = me
        self.core = lax.rem(me, 2)
        self.sib = me + 1 - 2 * self.core
        self.coord = [lax.rem(me // s, 4) for s in STRIDES]

    def near(self, axis, step):
        m = self.coord[axis]
        return self.me + (lax.rem(m + step, 4) - m) * STRIDES[axis]

    def hop(self, steps):
        return lax.rem(self.me + steps, 128)


class Copy:
    def __init__(self, src, dst, send, recv, dev):
        self.fields = dict(src_ref=src, dst_ref=dst, send_sem=send, recv_sem=recv, device_id=(dev,), device_id_type=MESH)

    def start(self):
        pltpu.make_async_remote_copy(**self.fields).start()

    def wait_send(self):
        pltpu.make_async_remote_copy(**self.fields).wait_send()

    def wait_recv(self):
        pltpu.make_async_remote_copy(**self.fields).wait_recv()


def rows_loop(total, step, body):
    def run(i, carry):
        body(pl.multiple_of(i * step, step))
        return carry

    lax.fori_loop(0, total // step, run, 0)


def peers(place):
    near = [place.near(a, s) for a in range(3) for s in (1, 2, 3)] + [place.sib]
    return near + [place.hop(s) for s in (21, 107, 64, 106, 22)]


def arrive(place):
    for device in peers(place):
        pl.semaphore_signal(pltpu.get_barrier_semaphore(), inc=1, device_id=(device,), device_id_type=MESH)


def all_arrived(place):
    pl.semaphore_wait(pltpu.get_barrier_semaphore(), len(peers(place)))


def sigmoid(v):
    return 1.0 / (1.0 + jnp.exp(-v))


def silu_slope(v):
    s = sigmoid(v)
    return s * (1.0 + v * (1.0 - s))


def rounded(v):
    return v.astype(BF16).astype(F32)


def dot(a, b):
    return jnp.dot(a, b, preferred_element_type=F32)


def dot_nt(a, b):
    return lax.dot_general(a, b, (((1,), (1,)), ((), ())), preferred_element_type=F32)


class Reduce:
    def __init__(self, refs):
        self.__dict__.update(refs)
        self.kinds = {}
        self.steps = (
            self.c0, self.s1, self.s1b, self.s2, self.s3, self.t3, self.t2, self.t1, self.t1b, self.t1c, self.t0,
            self.left, self.left_last, self.b0, self.b1,
        )

    def axes(self, p):
        return [p, (p + 1) % 3, (p + 2) % 3]

    def copy(self, c, p, kind, src, dst, dev):
        k = self.kinds.setdefault(kind, len(self.kinds))
        return Copy(src, dst, self.sends.at[c, p, k], self.recvs.at[c, p, k], dev)

    def span(self, core, block, start, size):
        return pl.ds(pl.multiple_of(core * 960 + block * 240 + start, 16), size)

    def d0(self, c, p):
        P = self.place
        far = pl.ds(pl.multiple_of((1 - P.core) * 960, 16), 960)
        return self.copy(c, p, "core", self.g.at[c, p, far], self.sib.at[c, p], P.sib)

    def d1(self, c, p):
        P = self.place
        ax = self.axes(p)[0]
        m = P.coord[ax]
        right, left, across = [lax.rem(m + d, 4) for d in (1, 3, 2)]
        dr, dl = P.near(ax, 1), P.near(ax, 3)
        first = lambda b: self.sib.at[c, p, self.span(0, b, 0, 128)]
        second = lambda b: self.sib.at[c, p, self.span(0, b, 128, 112)]
        h0, h1 = pl.ds(0, 128), pl.ds(128, 112)
        return dict(
            ar=self.copy(c, p, "1ar", first(across), self.r1o.at[c, p, 0], dr),
            al=self.copy(c, p, "1al", second(across), self.r1o.at[c, p, 1, pl.ds(0, 112)], dl),
            ra=self.copy(c, p, "1ra", second(right), self.r1.at[c, p, 0, h1], dr),
            la=self.copy(c, p, "1la", first(left), self.r1.at[c, p, 1, h0], dl),
            rb=self.copy(c, p, "1rb", first(right), self.r1.at[c, p, 0, h0], dr),
            lb=self.copy(c, p, "1lb", second(left), self.r1.at[c, p, 1, h1], dl),
        )

    def d2(self, c, p):
        P = self.place
        ax = self.axes(p)[1]
        return [
            self.copy(c, p, "2" + str(s), self.q1.at[c, p, lax.rem(P.coord[ax] + s, 4)], self.r2.at[c, p, s - 1], P.near(ax, s))
            for s in (2, 1, 3)
        ]

    def d3(self, c, p):
        P = self.place
        ax = self.axes(p)[2]
        return [
            self.copy(c, p, "3" + str(s), self.q2.at[c, p, lax.rem(P.coord[ax] + s, 4)], self.r3.at[c, p, s - 1], P.near(ax, s))
            for s in (2, 1, 3)
        ]

    def piece(self, p):
        second, third = self.axes(p)[1:]
        return pl.ds(pl.multiple_of(self.place.coord[second] * 64 + self.place.coord[third] * 16, 16), 16)

    def e3(self, c, p):
        third = self.axes(p)[2]
        mine = self.a2.at[c, p, self.piece(p)]
        return [self.copy(c, p, "e3" + str(s), mine, mine, self.place.near(third, s)) for s in (2, 1, 3)]

    def e2(self, c, p):
        second = self.axes(p)[1]
        mine = self.a2.at[c, p, pl.ds(pl.multiple_of(self.place.coord[second] * 64, 16), 64)]
        return [self.copy(c, p, "e2" + str(s), mine, mine, self.place.near(second, s)) for s in (2, 1, 3)]

    def e1(self, c, p):
        P = self.place
        ax = self.axes(p)[0]
        m = P.coord[ax]
        dr, dl = P.near(ax, 1), P.near(ax, 3)
        right, left, across = [lax.rem(m + d, 4) for d in (1, 3, 2)]
        block = lambda b: self.g.at[c, p, self.span(P.core, b, 0, 240)]
        first = lambda b: self.g.at[c, p, self.span(P.core, b, 0, 128)]
        second = lambda b: self.g.at[c, p, self.span(P.core, b, 128, 112)]
        src = self.a2.at[c, p, pl.ds(0, 240)]
        cp = functools.partial(self.copy, c, p)
        return dict(
            r=cp("e1r", src, block(m), dr),
            l=cp("e1l", src, block(m), dl),
            s=cp("e1s", src, block(m), P.sib),
            fr=cp("e1fr", first(left), first(left), dr),
            fl=cp("e1fl", second(right), second(right), dl),
            sr=cp("e1sr", block(right), block(right), P.sib),
            sl=cp("e1sl", block(left), block(left), P.sib),
            s0=cp("e1s0", first(across), first(across), P.sib),
            s1=cp("e1s1", second(across), second(across), P.sib),
        )

    def own(self, c, p):
        m = self.place.coord[self.axes(p)[0]]
        src = self.a2.at[c, p, pl.ds(0, 240)]
        return pltpu.make_async_copy(src, self.g.at[c, p, self.span(self.place.core, m, 0, 240)], self.local.at[c, p])

    def c0(self, c, p):
        self.d0(c, p).start()

    def s1(self, c, p):
        self.d0(c, p).wait_send()
        pl.semaphore_signal(self.free.at[c, p], inc=1, device_id=(self.place.sib,), device_id_type=MESH)
        self.d0(c, p).wait_recv()

        def add(r0):
            rows = pl.ds(r0, 48)
            mine = pl.ds(pl.multiple_of(self.place.core * 960 + r0, 16), 48)
            self.sib[c, p, rows, :] = (self.sib[c, p, rows, :].astype(F32) + self.g[c, p, mine, :].astype(F32)).astype(BF16)

        rows_loop(960, 48, add)
        d = self.d1(c, p)
        for k in ("ar", "al", "ra", "la"):
            d[k].start()

    def s1b(self, c, p):
        d = self.d1(c, p)
        m = self.place.coord[self.axes(p)[0]]
        right, left = lax.rem(m + 1, 4), lax.rem(m + 3, 4)

        def add(block, start, count, slot):
            def some(r0):
                to = pl.ds(pl.multiple_of(block * 240 + start + r0, 16), 16)
                part = self.r1o[c, p, slot, pl.ds(r0, 16), :].astype(F32)
                self.sib[c, p, to, :] = (self.sib[c, p, to, :].astype(F32) + part).astype(BF16)

            rows_loop(count, 16, some)

        d["ar"].wait_recv()
        add(right, 0, 128, 0)
        d["rb"].start()
        d["al"].wait_recv()
        add(left, 128, 112, 1)
        d["lb"].start()

    def s2(self, c, p):
        d = self.d1(c, p)
        m = self.place.coord[self.axes(p)[0]]
        for k in ("ra", "la", "rb", "lb"):
            d[k].wait_recv()

        def add(r0):
            rows = pl.ds(r0, 16)
            mine = pl.ds(pl.multiple_of(m * 240 + r0, 16), 16)
            total = self.sib[c, p, mine, :].astype(F32) + self.r1[c, p, 0, rows, :].astype(F32)
            total = total + self.r1[c, p, 1, rows, :].astype(F32)
            b = r0 // 64
            self.q1[c, p, b, pl.ds(pl.multiple_of(r0 - b * 64, 16), 16), :] = total.astype(BF16)

        rows_loop(240, 16, add)
        self.q1[c, p, 3, 48:64, :] = jnp.zeros((16, 640), BF16)
        for k in self.d2(c, p):
            k.start()

    def level2(self, c, p, b):
        m = self.place.coord[self.axes(p)[1]]
        rows = pl.ds(pl.multiple_of(b * 16, 16), 16)
        total = self.q1[c, p, m, rows, :].astype(F32)
        for s in range(3):
            total = total + self.r2[c, p, s, rows, :].astype(F32)
        return total

    def s3(self, c, p):
        for k in self.d2(c, p):
            k.wait_recv()

        def add(b, carry):
            self.q2[c, p, b] = self.level2(c, p, b).astype(BF16)
            return carry

        lax.fori_loop(0, 4, add, 0)
        for k in self.d3(c, p):
            k.start()

    def t3(self, c, p):
        for k in self.d3(c, p):
            k.wait_recv()
        total = self.level2(c, p, self.place.coord[self.axes(p)[2]])
        for s in range(3):
            total = total + self.r3[c, p, s].astype(F32)
        self.a2[c, p, self.piece(p), :] = total.astype(BF16)
        for k in self.e3(c, p):
            k.start()

    def t2(self, c, p):
        for k in self.e3(c, p):
            k.wait_recv()
        for k in self.e2(c, p):
            k.start()

    def t1(self, c, p):
        for k in self.e2(c, p):
            k.wait_recv()
        e = self.e1(c, p)
        e["r"].start()
        e["l"].start()
        pl.semaphore_wait(self.free.at[c, p], 1)
        e["s"].start()
        self.own(c, p).start()

    def t1b(self, c, p):
        e = self.e1(c, p)
        e["r"].wait_recv()
        e["fr"].start()
        e["sl"].start()
        e["l"].wait_recv()
        e["fl"].start()
        e["sr"].start()

    def t1c(self, c, p):
        e = self.e1(c, p)
        e["fr"].wait_recv()
        e["s0"].start()
        e["fl"].wait_recv()
        e["s1"].start()

    def t0(self, c, p):
        e = self.e1(c, p)
        for k in ("s", "sr", "sl", "s0", "s1"):
            e[k].wait_recv()
        self.own(c, p).wait()

    def bias_copies(self, level):
        P = self.place
        if level == 0:
            peers = [(0, P.sib, P.core)]
        else:
            peers = [(s, P.near(level - 1, s), P.coord[level - 1]) for s in (1, 2, 3)]
        return [
            self.copy(0, 0, "b%d%d" % (level, s), self.bias.at[level, slot], self.bias.at[level, slot], dev)
            for s, dev, slot in peers
        ]

    def b0(self, c, p):
        level = 3 * c + p
        for k in self.bias_copies(level):
            k.start()

    def b1(self, c, p):
        level = 3 * c + p
        for k in self.bias_copies(level):
            k.wait_recv()
        total = self.bias[level, 0] + self.bias[level, 1]
        if level:
            total = total + self.bias[level, 2] + self.bias[level, 3]
        if level < 3:
            self.bias[level + 1, self.place.coord[level]] = total
            self.b0((level + 1) // 3, (level + 1) % 3)
        else:
            self.bias_out[...] = total

    def left(self, c, p):
        for k in list(self.d1(c, p).values()) + self.d2(c, p) + self.d3(c, p) + self.e3(c, p) + self.e2(c, p):
            k.wait_send()

    def left_last(self, c, p):
        for k in self.e1(c, p).values():
            k.wait_send()

    def finish(self):
        for p in range(3):
            self.left_last(1, p)
        for level in range(4):
            for k in self.bias_copies(level):
                k.wait_send()


def reduce_scratch():
    v = lambda *s: pltpu.VMEM((2, 3) + s, BF16)
    sems = pltpu.SemaphoreType.DMA((2, 3, KINDS))
    return dict(
        sib=v(960, 640),
        r1=v(2, 240, 640),
        r1o=v(2, 128, 640),
        r2=v(3, 64, 640),
        r3=v(3, 16, 640),
        q1=v(4, 64, 640),
        q2=v(4, 16, 640),
        a2=v(256, 640),
        bias=pltpu.VMEM((4, 4, 8, 640), F32),
        sends=sems,
        recvs=sems,
        local=pltpu.SemaphoreType.DMA((2, 3)),
        free=pltpu.SemaphoreType.REGULAR((2, 3)),
    )


class Block:
    def __init__(self, refs):
        self.__dict__.update(refs)

    def load(self, which, r):
        src = (self.kernel_one, self.kernel_two)[which].at[r]
        return pltpu.make_async_copy(src, self.taps.at[r], self.tap_sems.at[r])

    def wait_taps(self, r):
        self.load(0, r).wait()

    def fetch(self, name):
        k = self.inputs.index(name)
        return pltpu.make_async_copy(getattr(self, name), getattr(self, name + "_v"), self.in_sems.at[k])

    def begin(self):
        zeros = jnp.zeros((16, 640), F32)
        self.borders()
        self.xp[0:8, :] = zeros[:8]
        self.xp[584:592, :] = zeros[:8]
        for start in (0, 80, 160):
            self.xs[start : start + 16, :] = zeros[:16]
        self.xl[0:16, :] = zeros[:16]
        self.xl[160:176, :] = zeros[:16]

        def edges(base, count, column):
            n = lax.broadcasted_iota(jnp.int32, (count, 128), 0)
            j, last = column(n)
            self.edge[0, base : base + count, :] = jnp.where(j > 0, 1.0, 0.0)
            self.edge[1, base : base + count, :] = jnp.where(j < last, 1.0, 0.0)

        def twelfth(n):
            return (n * 43691) >> 19

        def wide(n):
            return n - 12 * twelfth(n), 11

        edges(0, 576, lambda n: wide(n >> 2))
        edges(576, 128, lambda n: (n & 7, 7))
        edges(704, 144, wide)
        n = lax.broadcasted_iota(jnp.int32, (576, 128), 0)
        cell = n >> 2
        i = twelfth(cell)
        j = cell - 12 * i
        keep = jnp.where((i < 8) & (j < 8), 1.0, 0.0)
        for m in range(4):
            group = jnp.where(self.group[m] == 1, 1.0, 0.0)
            keep = jnp.maximum(keep, jnp.where((n & 3) == m, group, 0.0))
        self.region[...] = keep

    def borders(self):
        self.cols[0:48, :] = jnp.zeros((48, 1920), BF16)
        self.cols[624:672, :] = jnp.zeros((48, 1920), BF16)

    def train_cols(self, sign):
        for q in range(3):
            dj = sign * (q - 1)
            v = self.xp[pl.ds(8 + dj * 4, 576), :]
            if dj:
                v = v * self.edge[(dj + 1) // 2, 0:576, 0:1]
            self.cols[48:624, q * 640 : (q + 1) * 640] = v.astype(BF16)

    def chain_cols(self, sign):
        for r in range(3):
            self.chain_row(r, sign, self.cols.at[pl.ds(272 * r, 272)])

    def chain_row(self, r, sign, cols):
        for q in range(3):
            dj = sign * (q - 1)
            to = pl.ds(q * 640, 640)
            for m in range(2):
                v = self.xs[pl.ds(16 + 80 * m + sign * (r - 1) * 8 + dj, 64), :]
                if dj:
                    v = v * self.edge[(dj + 1) // 2, 576 + 64 * m : 640 + 64 * m, 0:1]
                cols[64 * m : 64 * m + 64, to] = v.astype(BF16)
            v = self.xl[pl.ds(16 + sign * (r - 1) * 12 + dj, 144), :]
            if dj:
                v = v * self.edge[(dj + 1) // 2, 704:848, 0:1]
            cols[128:272, to] = v.astype(BF16)

    def clear(self):
        self.acc[...] = jnp.zeros((576, 640), F32)

    def product(self, r, rows, back, cols):
        taps = self.taps.at[r]
        if back:
            total = None
            for q in range(3):
                cut = pl.ds(q * 640, 640)
                part = dot_nt(cols[:, cut], taps[cut, :])
                total = part if total is None else total + part
        else:
            total = dot(cols[...], taps[...])
        self.acc[0:rows, :] += total

    def train_side(self, r, sign):
        return self.cols.at[pl.ds(pl.multiple_of(48 + sign * (r - 1) * 48, 16), 576)]

    def train_conv(self, back, wait, then, r):
        if wait:
            self.wait_taps(r)
        self.product(r, 576, back, self.train_side(r, -1 if back else 1))
        if then is not None:
            self.load(then, r).start()

    def chain_conv(self, back, wait, then, r):
        if wait is not None:

            @pl.when(wait)
            def _():
                self.wait_taps(r)

        self.product(r, 272, back, self.cols.at[pl.ds(pl.multiple_of(272 * r, 16), 272)])
        if then is not None:
            self.load(then, r).start()

    def train_wgrad(self, chunk, r):
        side = self.train_side(r, -1)
        for start, size in ((0, 768), (768, 768), (1536, 384)):
            part = dot(self.turned[...], side[:, start : start + size]).astype(BF16)
            for q in range(3):
                low, high = max(start, q * 640), min(start + size, q * 640 + 640)
                if low < high:
                    self.g[chunk, r, q * 640 : q * 640 + 640, low - q * 640 : high - q * 640] = part[:, low - start : high - start]

    def map_rows(self, ref, r0):
        return ref[pl.ds(r0 // 4, 12)].astype(F32).reshape(48, 640)

    def train_start(self):
        self.fetch("maps").wait()
        def some(r0):
            rows = pl.ds(r0, 48)
            v = self.map_rows(self.maps_v, r0)
            a = (v * sigmoid(v) * self.region[rows, 0:1]).astype(BF16)
            self.low_in[rows, :] = a
            self.xp[pl.ds(pl.multiple_of(r0 + 8, 8), 48), :] = a.astype(F32)

        rows_loop(576, 48, some)
        self.train_cols(1)
        self.clear()

    def train_middle(self):
        self.fetch("cot").wait()
        self.sums[...] = jnp.zeros((8, 640), F32)

        def some(r0):
            rows = pl.ds(r0, 48)
            v = self.acc[rows, :] + self.bias_one[...].reshape(1, 640)
            keep = self.region[rows, 0:1]
            self.low_mid[rows, :] = (v * sigmoid(v) * keep).astype(BF16)
            self.pre_one[rows, :] = silu_slope(v) * keep
            c = self.map_rows(self.cot_v, r0) * keep
            self.xp[pl.ds(pl.multiple_of(r0 + 8, 8), 48), :] = c
            self.sums[1:2, :] += jnp.sum(c, axis=0, keepdims=True)

        rows_loop(576, 48, some)
        self.turned[...] = self.low_mid[...].T
        self.train_cols(-1)
        self.clear()

    def train_back(self):
        def some(r0):
            rows = pl.ds(r0, 48)
            v = rounded(self.acc[rows, :] * self.pre_one[rows, :])
            self.xp[pl.ds(pl.multiple_of(r0 + 8, 8), 48), :] = v
            self.sums[0:1, :] += jnp.sum(v, axis=0, keepdims=True)

        rows_loop(576, 48, some)
        self.turned[...] = self.low_in[...].T
        self.bias[0, self.place.core] = self.sums[...]
        self.train_cols(-1)

    def put_xp(self, low):
        def some(r0):
            rows = pl.ds(r0, 48)
            self.xp[pl.ds(pl.multiple_of(r0 + 8, 8), 48), :] = low[rows, :].astype(F32)

        rows_loop(576, 48, some)
        self.train_cols(1)
        self.clear()

    def train_grad_end(self):
        def some(r0):
            rows = pl.ds(r0, 48)
            keep = self.region[rows, 0:1]
            slope = silu_slope(self.map_rows(self.maps_v, r0)) * keep
            self.acc[rows, :] = self.map_rows(self.cot_v, r0) * keep + self.acc[rows, :] * slope

        rows_loop(576, 48, some)
        self.grad[...] = self.acc[...].reshape(144, 4, 640)

    def train_out_end(self):
        def some(r0):
            rows = pl.ds(r0, 48)
            v = self.map_rows(self.maps_v, r0) + (self.acc[rows, :] + self.bias_two[...].reshape(1, 640))
            self.acc[rows, :] = v * self.region[rows, 0:1]

        rows_loop(576, 48, some)
        self.out[...] = self.acc[...].astype(BF16).reshape(144, 4, 640)

    def chain_peers(self):
        P = self.place
        pairs = []
        for s in range(2):
            cut = pl.ds(8 * s, 8)
            pairs.append((s, self.chosen_small.at[cut], self.arrived_small.at[cut], self.samples_small.at[cut], self.ret_small.at[cut], SMALL_HOPS[s]))
        pairs.append((2, self.chosen_large, self.arrived_large, self.samples_large, self.ret_large, LARGE_HOP))
        there = [Copy(a, b, self.go_sems.at[0, k], self.go_sems.at[1, k], P.hop(h)) for k, a, b, _, _, h in pairs]
        back = [Copy(a, b, self.go_sems.at[2, k], self.go_sems.at[3, k], P.hop(128 - h)) for k, _, _, a, b, h in pairs]
        return there, back

    def buffers(self):
        return [
            pltpu.make_async_copy(self.buffer_small, self.g.at[1, 0, pl.ds(0, 1024)], self.buffer_sems.at[0]),
            pltpu.make_async_copy(self.buffer_large, self.g.at[1, 1, pl.ds(0, 1152)], self.buffer_sems.at[1]),
        ]

    def chain_send(self):
        all_arrived(self.place)
        for k in self.buffers():
            k.wait()
        n = lax.broadcasted_iota(jnp.int32, (128, 1024), 0)
        at = lax.broadcasted_iota(jnp.int32, (128, 1024), 1)
        start = jnp.where(n < 64, self.fetch_small[0], self.fetch_small[1]) * 64
        pick = jnp.where(at == start + (n & 63), 1.0, 0.0).astype(BF16)
        rows = dot(pick, self.g[1, 0, 0:1024, :]).astype(BF16)
        self.chosen_small[...] = rows.reshape(16, 8, 640)
        n = lax.broadcasted_iota(jnp.int32, (144, 1152), 0)
        at = lax.broadcasted_iota(jnp.int32, (144, 1152), 1)
        pick = jnp.where(at == n * 8 + self.fetch_large[0], 1.0, 0.0).astype(BF16)
        rows = dot(pick, self.g[1, 1, 0:1152, :]).astype(BF16)
        for i in range(12):
            self.chosen_large[i] = rows[12 * i : 12 * i + 12]
        for k in self.chain_peers()[0]:
            k.start()

    def flat_small(self, ref):
        return ref.astype(F32).reshape(128, 640)

    def spread(self, value):
        for m in range(2):

            def small(r0, m=m):
                self.xs[pl.ds(pl.multiple_of(16 + 80 * m + r0, 8), 16), :] = value(pl.multiple_of(64 * m + r0, 16))

            rows_loop(64, 16, small)

        def large(r0):
            self.xl[pl.ds(pl.multiple_of(16 + r0, 8), 16), :] = value(pl.multiple_of(128 + r0, 16))

        rows_loop(144, 16, large)

    def chain_start(self):
        for name in ("probe_small", "probe_large"):
            self.fetch(name).wait()
        self.probe[0:128, :] = self.flat_small(self.probe_small_v[...])
        for i in range(12):
            self.probe[128 + 12 * i : 140 + 12 * i, :] = self.probe_large_v[i].astype(F32)
        self.spread(lambda r0: self.probe[pl.ds(r0, 16), :])
        self.chain_cols(-1)
        self.clear()

    def chain_state(self):
        for name in ("fresh_small", "fresh_large", "noise_small", "noise_large"):
            self.fetch(name).wait()
        for k in self.chain_peers()[0]:
            k.wait_recv()
        for s in range(2):
            fresh = jnp.where(self.reinit_small[s] == 1, 1.0, 0.0)
            cut = slice(8 * s, 8 * s + 8)
            v = self.fresh_small_v[cut].astype(F32) * fresh + self.arrived_small[cut].astype(F32) * (1.0 - fresh)
            self.state[64 * s : 64 * s + 64, :] = v.reshape(64, 640)
        fresh = jnp.where(self.reinit_large[0] == 1, 1.0, 0.0)
        for i in range(12):
            v = self.fresh_large_v[i].astype(F32) * fresh + self.arrived_large[i].astype(F32) * (1.0 - fresh)
            self.state[128 + 12 * i : 140 + 12 * i, :] = v

    def chain_kept(self):
        self.slope_in[...] = self.acc[0:272, :]

    def chain_act(self):
        def value(r0):
            v = self.state[pl.ds(r0, 16), :]
            return rounded(v * sigmoid(v))

        self.spread(value)
        self.chain_cols(1)
        self.clear()

    def chain_mid(self):
        def value(r0):
            rows = pl.ds(r0, 16)
            v = self.acc[rows, :] + self.bias_one[...].reshape(1, 640)
            return rounded(silu_slope(v) * self.slope_in[rows, :])

        self.spread(value)
        self.chain_cols(-1)
        self.clear()

    def chain_step(self, t):
        late = jnp.where(t == 1, 1.0, 0.0)
        early = 1.0 - late

        def small(r0):
            rows = pl.ds(r0, 16)
            v = self.state[rows, :]
            noise = self.noise_small_v[t, pl.ds(r0 // 8, 2)].astype(F32).reshape(16, 640)
            self.state[rows, :] = v + (self.probe[rows, :] + silu_slope(v) * self.acc[rows, :]) + noise

        rows_loop(128, 16, small)

        def large(r0):
            rows = pl.ds(pl.multiple_of(128 + r0, 16), 16)
            v = self.state[rows, :]
            noise = self.noise_large_v[pl.ds(r0, 16)].astype(F32)
            noise = noise[:, 0, :] * early + noise[:, 1, :] * late
            self.state[rows, :] = v + (self.probe[rows, :] + silu_slope(v) * self.acc[rows, :]) + noise

        rows_loop(144, 16, large)

    def chain_end(self):
        self.samples_small[...] = self.state[0:128, :].astype(BF16).reshape(16, 8, 640)
        for i in range(12):
            self.samples_large[i] = self.state[128 + 12 * i : 140 + 12 * i, :].astype(BF16)
        for k in self.chain_peers()[1]:
            k.start()
        self.borders()
        self.train_cols(-1)
        self.clear()

    def finish(self):
        there, back = self.chain_peers()
        for k in back:
            k.wait_recv()
        for k in there + back:
            k.wait_send()


INPUTS = (
    "maps", "cot", "probe_small", "probe_large", "fresh_small", "fresh_large", "noise_small", "noise_large",
)
OUTPUTS = ("samples_small", "samples_large", "out", "grad")
INPUT_SHAPES = (
    (144, 4, 640), (144, 4, 640), (16, 8, 640), (12, 12, 640), (16, 8, 640), (12, 12, 640), (2, 16, 8, 640), (144, 2, 640),
)


def block_scratch():
    f = lambda *s: pltpu.VMEM(s, F32)
    b = lambda *s: pltpu.VMEM(s, BF16)
    dma = pltpu.SemaphoreType.DMA
    found = {name + "_v": b(*shape) for name, shape in zip(INPUTS, INPUT_SHAPES)}
    found.update(
        taps=b(3, 1920, 640),
        cols=b(816, 1920),
        xp=f(592, 640),
        xs=f(176, 640),
        xl=f(176, 640),
        acc=f(576, 640),
        pre_one=f(576, 640),
        low_in=b(576, 640),
        low_mid=b(576, 640),
        turned=b(640, 576),
        edge=f(2, 848, 128),
        region=f(576, 128),
        sums=f(8, 640),
        probe=f(272, 640),
        state=f(272, 640),
        slope_in=f(272, 640),
        arrived_small=b(16, 8, 640),
        arrived_large=b(12, 12, 640),
        chosen_small=b(16, 8, 640),
        chosen_large=b(12, 12, 640),
        tap_sems=dma((3,)),
        in_sems=dma((len(INPUTS),)),
        buffer_sems=dma((2,)),
        go_sems=dma((4, 3)),
    )
    return found


class Loop:
    def __init__(self, count, body):
        self.count, self.body = count, body


def length(items):
    return sum(i.count * length(i.body(None)) if isinstance(i, Loop) else 1 for i in items)


def schedule(block):
    part = functools.partial

    def conv(back, wait=False, then=None):
        return Loop(3, lambda r: [part(block.train_conv, back, wait, then, r)])

    def chain(back, wait=None, then=None):
        return Loop(3, lambda r: [part(block.chain_conv, back, wait, then, r)])

    def wgrad(chunk):
        return Loop(3, lambda r: [part(block.train_wgrad, chunk, r)])

    def chain_turn(t):
        first = None if t is None else t == 0
        return [block.chain_act, chain(False, wait=first), block.chain_mid, chain(True), part(block.chain_step, t)]

    return [
        block.train_start,
        conv(False, wait=True, then=1),
        block.chain_send,
        block.train_middle,
        wgrad(0),
        conv(True, wait=True),
        block.train_back,
        wgrad(1),
        block.chain_start,
        chain(True, then=0),
        block.chain_kept,
        block.chain_state,
        Loop(2, chain_turn),
        block.chain_end,
        conv(True, then=1),
        block.train_grad_end,
        part(block.put_xp, block.low_mid),
        conv(False, wait=True),
        block.train_out_end,
    ]


def play(items, places, tick):
    done = 0
    for item in items:
        if isinstance(item, Loop):
            size = length(item.body(None))

            def turn(i, carry, item=item, size=size, done=done):
                inner = []
                for condition, base in places:
                    for k in range(item.count):
                        now = i == k
                        inner.append((now if condition is None else condition & now, base + done + k * size))
                play(item.body(i), inner, tick)
                return carry

            lax.fori_loop(0, item.count, turn, 0)
            done += item.count * size
        else:
            item()
            for condition, base in places:
                tick(condition, base + done)
            done += 1


TICKS = {
    6: (0,),
    7: (1,),
    8: (6, 2,),
    9: (7,),
    10: (8,),
    11: (12,),
    12: (78,),
    13: (13, 3,),
    14: (14, 4, 18, 9,),
    15: (5, 19, 84,),
    16: (10,),
    17: (11, 15,),
    18: (24,),
    19: (25, 20, 85,),
    21: (16,),
    22: (21, 17,),
    23: (86,),
    24: (30, 26, 22, 31,),
    26: (23, 32, 27,),
    27: (37, 36, 87,),
    28: (28, 38,),
    30: (29, 33,),
    31: (34,),
    32: (42,),
    33: (35, 39, 43,),
    34: (40, 44,),
    37: (41,),
    38: (45, 46, 48,),
    41: (47,),
    43: (50,),
    45: (49, 51,),
    46: (52, 53,),
    47: (54, 56, 55, 57,),
    48: (58, 63, 61, 59,),
    49: (66, 67, 68, 69, 70, 71, 72, 73, 74, 64, 60, 62, 65,),
}

B_INPUTS = INPUTS + (
    "buffer_small", "buffer_large", "kernel_one", "kernel_two",
    "group", "reinit_small", "reinit_large", "fetch_small", "fetch_large", "bias_one", "bias_two",
)
B_OUTPUTS = ("g",) + OUTPUTS + ("ret_small", "ret_large", "bias_out")


def block_kernel(names, *given):
    refs = dict(zip(names, given))
    refs.update(place=Place(), inputs=INPUTS)
    block, reduce = Block(refs), Reduce(refs)
    arrive(block.place)
    block.fetch("maps").start()
    for r in range(3):
        block.load(0, r).start()
    for k in block.buffers():
        k.start()
    for name in INPUTS[1:]:
        block.fetch(name).start()
    block.begin()

    def tick(condition, n):
        def run():
            for code in TICKS.get(n, ()):
                reduce.steps[code // 6](code // 3 % 2, code % 3)

        if condition is None:
            run()
        elif n in TICKS:
            pl.when(condition)(run)

    play(schedule(block), [(None, 0)], tick)
    block.finish()
    reduce.finish()


ANYWHERE = pl.BlockSpec(memory_space=pl.ANY)
SCALARS = pl.BlockSpec(memory_space=pltpu.SMEM)
INSIDE = pl.BlockSpec(memory_space=pltpu.VMEM)


def run_block(*args):
    scratch = reduce_scratch()
    scratch.update(block_scratch())
    names = B_INPUTS + B_OUTPUTS + tuple(scratch)
    held = [pltpu.with_memory_space_constraint(a, pltpu.HBM) if k < 12 else a for k, a in enumerate(args)]
    return pl.pallas_call(
        functools.partial(block_kernel, names),
        out_shape=(
            pltpu.VMEM((2, 3, 1920, 640), BF16),
            pltpu.VMEM((16, 8, 640), BF16),
            pltpu.VMEM((12, 12, 640), BF16),
            pltpu.VMEM((144, 4, 640), BF16),
            pltpu.VMEM((144, 4, 640), F32),
            pltpu.VMEM((16, 8, 640), BF16),
            pltpu.VMEM((12, 12, 640), BF16),
            pltpu.VMEM((8, 640), F32),
        ),
        in_specs=[ANYWHERE] * 12 + [SCALARS] * 5 + [INSIDE] * 2,
        out_specs=(INSIDE,) * 8,
        scratch_shapes=list(scratch.values()),
        compiler_params=pltpu.CompilerParams(collective_id=0, has_side_effects=True, vmem_limit_bytes=46 * 2**20),
        cost_estimate=pl.CostEstimate(flops=36 * 10**9, bytes_accessed=80 * 2**20, transcendentals=0),
    )(*held)


END_INPUTS = (
    "g", "samples_small_in", "samples_large_in", "out_in", "grad_in", "ret_small", "ret_large", "bias",
    "buffer_small", "buffer_large", "fetch_small", "fetch_large",
)
END_OUTPUTS = (
    "kernel_one", "kernel_two", "samples_small", "samples_large", "out", "grad", "new_small", "new_large", "bias_one", "bias_two",
)
END_SCRATCH = ("wide", "small", "large", "wide_sems", "sems")
PASSED = ("out", "grad", "samples_small", "samples_large")
CUT = 480
SLOTS = 4


def end_kernel(*given):
    r = dict(zip(END_INPUTS + END_OUTPUTS + END_SCRATCH, given))
    sems = r["sems"]
    small = pltpu.make_async_copy(r["buffer_small"], r["small"], sems.at[4])
    large = pltpu.make_async_copy(r["buffer_large"], r["large"], sems.at[5])
    small.start()
    large.start()
    passed = [pltpu.make_async_copy(r[n + "_in"], r[n], sems.at[k]) for k, n in enumerate(PASSED)]
    per_part = 1920 // CUT
    pending = []
    for n in range(6 * per_part):
        c, part, block = n // (3 * per_part), n // per_part % 3, n % per_part
        slot = n % SLOTS
        target = r["kernel_one"] if c else r["kernel_two"]
        copy = pltpu.make_async_copy(
            r["wide"].at[slot], target.at[pl.ds(part * 1920 + block * CUT, CUT)], r["wide_sems"].at[slot]
        )
        if n >= SLOTS:
            pending[n - SLOTS].wait()

        def some(r0):
            rows = pl.ds(pl.multiple_of(block * CUT + r0, 16), 96)
            r["wide"][slot, pl.ds(r0, 96), :] = r["g"][c, part, rows, :].astype(F32)

        rows_loop(CUT, 96, some)
        copy.start()
        pending.append(copy)
        if n == 0:
            for k in passed:
                k.start()
            r["bias_one"][...] = r["bias"][0, :]
            r["bias_two"][...] = r["bias"][1, :]
        if n == per_part:
            small.wait()
            for s in range(2):
                r["small"][r["fetch_small"][s]] = r["ret_small"][8 * s : 8 * s + 8]
            small = pltpu.make_async_copy(r["small"], r["new_small"], sems.at[4])
            small.start()
        if n == 2 * per_part:
            large.wait()
            chosen = lax.broadcasted_iota(jnp.int32, (12, 8, 640), 1) == r["fetch_large"][0]
            for i in range(12):
                cut = slice(12 * i, 12 * i + 12)
                new = jnp.broadcast_to(r["ret_large"][i].astype(F32)[:, None, :], (12, 8, 640))
                r["large"][cut] = jnp.where(chosen, new, r["large"][cut].astype(F32)).astype(BF16)
            large = pltpu.make_async_copy(r["large"], r["new_large"], sems.at[5])
            large.start()
    for k in pending[-SLOTS:] + passed + [small, large]:
        k.wait()


def run_end(*args):
    shape = pltpu.HBM
    held = [pltpu.with_memory_space_constraint(a, pltpu.HBM) if k in (8, 9) else a for k, a in enumerate(args)]
    return pl.pallas_call(
        end_kernel,
        out_shape=(
            shape((5760, 640), F32),
            shape((5760, 640), F32),
            shape((16, 8, 640), BF16),
            shape((12, 12, 640), BF16),
            shape((144, 4, 640), BF16),
            shape((144, 4, 640), F32),
            shape((16, 8, 8, 640), BF16),
            shape((144, 8, 640), BF16),
            jax.ShapeDtypeStruct((640,), F32),
            jax.ShapeDtypeStruct((640,), F32),
        ),
        in_specs=[INSIDE] * 8 + [ANYWHERE] * 2 + [SCALARS] * 2,
        out_specs=(ANYWHERE,) * 8 + (INSIDE,) * 2,
        scratch_shapes=[
            pltpu.VMEM((SLOTS, CUT, 640), F32),
            pltpu.VMEM((16, 8, 8, 640), BF16),
            pltpu.VMEM((144, 8, 640), BF16),
            pltpu.SemaphoreType.DMA((SLOTS,)),
            pltpu.SemaphoreType.DMA((6,)),
        ],
        compiler_params=pltpu.CompilerParams(vmem_limit_bytes=16 * 2**20),
    )(*held)


def map_minor(v):
    return v.transpose(1, 2, 0, 3).reshape(144, v.shape[0], 640)


def map_major(v):
    return v.reshape(12, 12, v.shape[1], 640).transpose(2, 0, 1, 3)


def local(
    buffer_small,
    buffer_large,
    fetch_small,
    fetch_large,
    reinit_small,
    reinit_large,
    fresh_small,
    fresh_large,
    noise_small,
    noise_large,
    probe_small,
    probe_large,
    train_maps,
    train_group,
    train_cot,
    kernel_one,
    bias_one,
    kernel_two,
    bias_two,
):
    g, samples_small, samples_large, out, grad, ret_small, ret_large, bias = run_block(
        map_minor(train_maps),
        map_minor(train_cot),
        probe_small.reshape(16, 8, 640),
        probe_large.reshape(12, 12, 640),
        fresh_small.reshape(16, 8, 640),
        fresh_large.reshape(12, 12, 640),
        noise_small.reshape(2, 16, 8, 640),
        noise_large.transpose(1, 2, 3, 0, 4).reshape(144, 2, 640),
        buffer_small.reshape(1024, 640),
        map_minor(buffer_large).reshape(1152, 640),
        kernel_one.reshape(3, 1920, 640),
        kernel_two.reshape(3, 1920, 640),
        train_group,
        reinit_small,
        reinit_large,
        fetch_small,
        fetch_large,
        bias_one,
        bias_two,
    )
    sums = run_end(
        g, samples_small, samples_large, out, grad, ret_small, ret_large, bias,
        buffer_small, map_minor(buffer_large), fetch_small, fetch_large,
    )
    sum_one, sum_two, samples_small, samples_large, out, grad, new_small, new_large, bias_sum_one, bias_sum_two = sums
    return (
        samples_small.reshape(2, 8, 8, 640),
        samples_large.reshape(1, 12, 12, 640),
        new_small,
        map_major(new_large),
        map_major(out),
        map_major(grad),
        sum_one.reshape(3, 3, 640, 640),
        bias_sum_one,
        sum_two.reshape(3, 3, 640, 640),
        bias_sum_two,
    )


def solution(mesh):
    in_specs = (
        P("dp", None, None, None),
        P("dp", None, None, None),
        P("dp"),
        P("dp"),
        P("dp"),
        P("dp"),
        P("dp", None, None, None),
        P("dp", None, None, None),
        P(None, "dp", None, None, None),
        P(None, "dp", None, None, None),
        P("dp", None, None, None),
        P("dp", None, None, None),
        P("dp", None, None, None),
        P("dp"),
        P("dp", None, None, None),
        P(),
        P(),
        P(),
        P(),
    )
    out_specs = (
        P("dp", None, None, None),
        P("dp", None, None, None),
        P("dp", None, None, None),
        P("dp", None, None, None),
        P("dp", None, None, None),
        P("dp", None, None, None),
        P(),
        P(),
        P(),
        P(),
    )
    return jax.shard_map(local, mesh=mesh, in_specs=in_specs, out_specs=out_specs, check_vma=False)
```
